32 devices in a mesh: section: 2 (over y), dp: 16 (over z, x, core).
Axes of the slice: x: 2, y: 2, z: 4, core: 2. Of those that a mesh axis runs over, the one named last changes fastest.
Arguments:
- latents: bfloat16 [2, 16, 5, 64, 1024], P(None, 'dp', None, None, 'section'), may hold values from -6 to 6
- media_tokens: bfloat16 [2, 16, 5, 256, 1024], P(None, 'dp', None, None, 'section'), may hold values from -6 to 6
- image_counts: int32 [2, 16], P(None, 'dp'), may hold values from 1 to 5, as said below
- cotangent: bfloat16 [2, 16, 5, 64, 1024], P(None, 'dp', None, None, 'section'), may hold values from -6 to 6
- query_weight: bfloat16 [2, 1024, 512], P('section'), may hold values from -0.1875 to 0.1875
- key_weight: bfloat16 [2, 1024, 512], P('section'), may hold values from -0.1875 to 0.1875
- value_weight: bfloat16 [2, 1024, 512], P('section'), may hold values from -0.1875 to 0.1875
- output_weight: bfloat16 [2, 512, 1024], P('section'), may hold values from -6 to 6
- up_weight: bfloat16 [2, 1024, 4096], P('section'), may hold values from -0.1875 to 0.1875
- down_weight: bfloat16 [2, 4096, 1024], P('section'), may hold values from -0.09375 to 0.09375
- media_gain: float32 [2, 1024], P('section'), may hold values from 0.5 to 1.5
- media_bias: float32 [2, 1024], P('section'), may hold values from -1 to 1
- latent_gain: float32 [2, 1024], P('section'), may hold values from 0.5 to 1.5
- latent_bias: float32 [2, 1024], P('section'), may hold values from -1 to 1
- feed_gain: float32 [2, 1024], P('section'), may hold values from 0.5 to 1.5
- feed_bias: float32 [2, 1024], P('section'), may hold values from -1 to 1
Outputs:
- resampled: bfloat16 [2, 16, 5, 64, 1024], P(None, 'dp', None, None, 'section')
- latent_grad: float32 [2, 16, 5, 64, 1024], P(None, 'dp', None, None, 'section')
- media_grad: float32 [2, 16, 5, 256, 1024], P(None, 'dp', None, None, 'section')
- query_grad: float32 [2, 1024, 512], P('section', None, 'dp')
- key_grad: float32 [2, 1024, 512], P('section', None, 'dp')
- value_grad: float32 [2, 1024, 512], P('section', None, 'dp')
- output_grad: float32 [2, 512, 1024], P('section', None, 'dp')
- up_grad: float32 [2, 1024, 4096], P('section', None, 'dp')
- down_grad: float32 [2, 4096, 1024], P('section', None, 'dp')
- media_gain_grad: float32 [2, 1024], P('section', 'dp')
- media_bias_grad: float32 [2, 1024], P('section', 'dp')
- latent_gain_grad: float32 [2, 1024], P('section', 'dp')
- latent_bias_grad: float32 [2, 1024], P('section', 'dp')
- feed_gain_grad: float32 [2, 1024], P('section', 'dp')
- feed_bias_grad: float32 [2, 1024], P('section', 'dp')
The draws below stay inside these ranges and needn't reach their ends.
Inputs may be any that keep to these rules, and one draw needn't show every extreme that they name: Sample b of micro-batch j holds its images in slots 0 to image_counts[j, b] - 1; the later slots of that sample are padding.
All inputs are finite; a program needn't handle non-finite values.
Results may differ from the reference program's by a relative error of at most 0.02.
Values may be sent and summed in bfloat16 or wider, within the bound.
A program may use at most 448 MiB of HBM per device.

```python
import jax
import jax.numpy as jnp
from jax import lax

D = 1024
DH = 64
INNER = 512
FF = 4096
LAT = 64
PATCH = 256
SLOTS = 5
MB = 2
SAMPLES = 16


def draw_image_counts(key, part):
    key = jax.random.fold_in(key, 7)
    count_key, place_key, other_key = jax.random.split(key, 3)
    entries = MB * SAMPLES
    counts_flat = jax.random.randint(count_key, (entries,), 1, SLOTS + 1)
    high_spot = jax.random.randint(place_key, (), 0, entries)
    low_spot = (high_spot + 1 + jax.random.randint(other_key, (), 0, entries - 1)) % entries
    counts_flat = counts_flat.at[high_spot].set(SLOTS).at[low_spot].set(1)
    return counts_flat.reshape(MB, SAMPLES).astype(jnp.int32)


def spiked(array, stream_key, source, target, parts, factor):
    def block_of(axis_at):
        return (jnp.arange(array.shape[axis_at]) // (array.shape[axis_at] // parts)).reshape((-1,) + (1,) * (array.ndim - 1 - axis_at))

    first = jax.random.permutation(stream_key, parts)[block_of(target)]
    far = (block_of(target) + parts // 2) % parts
    return jnp.where((block_of(source) == first) | (block_of(source) == far), factor * array, array)


def steps_of(rng, shape, shards, smallest, largest):
    level, own = 1.0, jax.random.fold_in(rng, 6)
    for dim, parts in shards:
        steps = jnp.exp(jax.random.uniform(jax.random.fold_in(own, dim), (parts,), jnp.float32, smallest / len(shards), largest / len(shards)))
        level = level * jnp.repeat(steps, shape[dim] // parts).reshape([-1 if axis == dim else 1 for axis in range(len(shape))])
    return level


def scatter_about(key, extent, width, reach, shards=(), dtype=jnp.bfloat16):
    factor_of = steps_of(key, extent, shards, -0.22, 0.18) if shards else 1.0
    values = jax.random.normal(key, extent, jnp.float32) * width * factor_of
    return jnp.minimum(jnp.maximum(values, -reach), reach).astype(dtype)


def heavy_noise(stream_key, extent, spread, limit, cuts, heavy, dtype=jnp.bfloat16):
    array = spread * jax.random.normal(stream_key, extent, jnp.float32)
    if cuts:
        array = array * steps_of(stream_key, extent, cuts, -0.22, 0.18)
    return jnp.clip(spiked(array, jax.random.fold_in(stream_key, 3), *heavy), -limit, limit).astype(dtype)


def setup_inputs(seed: int = 0) -> dict:
    arg_keys = jax.random.split(jax.random.key(seed), 17)
    return {
        "latents": scatter_about(arg_keys[0], (MB, SAMPLES, SLOTS, LAT, D), 1.0, 6.0, ((1, 16), (4, 2))),
        "media_tokens": scatter_about(arg_keys[1], (MB, SAMPLES, SLOTS, PATCH, D), 1.0, 6.0, ((1, 16), (4, 2))),
        "image_counts": draw_image_counts(jax.random.fold_in(arg_keys[16], 71), 0),
        "cotangent": heavy_noise(arg_keys[3], (MB, SAMPLES, SLOTS, LAT, D), 1.0, 6.0, ((1, 16), (4, 2)), (1, 4, 16, 2.0)),
        "query_weight": scatter_about(arg_keys[4], (2, D, INNER), D ** -0.5, 0.1875, ((0, 2),)),
        "key_weight": scatter_about(arg_keys[5], (2, D, INNER), D ** -0.5, 0.1875, ((0, 2),)),
        "value_weight": scatter_about(arg_keys[6], (2, D, INNER), D ** -0.5, 0.1875, ((0, 2),)),
        "output_weight": scatter_about(arg_keys[7], (2, INNER, D), (max(INNER // (PATCH + LAT), 1)) ** -0.5, 6.0, ((0, 2),)),
        "up_weight": scatter_about(arg_keys[8], (2, D, FF), D ** -0.5, 0.1875, ((0, 2),)),
        "down_weight": scatter_about(arg_keys[9], (2, FF, D), FF ** -0.5, 0.09375, ((0, 2),)),
        "media_gain": jnp.clip(1.0 + 0.1 * jax.random.normal(arg_keys[10], (2, D), jnp.float32), 0.5, 1.5),
        "media_bias": scatter_about(arg_keys[11], (2, D), 0.2, 1.0, ((0, 2),), jnp.float32),
        "latent_gain": jnp.clip(1.0 + 0.1 * jax.random.normal(arg_keys[12], (2, D), jnp.float32), 0.5, 1.5),
        "latent_bias": scatter_about(arg_keys[13], (2, D), 0.2, 1.0, ((0, 2),), jnp.float32),
        "feed_gain": jnp.clip(1.0 + 0.1 * jax.random.normal(arg_keys[14], (2, D), jnp.float32), 0.5, 1.5),
        "feed_bias": scatter_about(arg_keys[15], (2, D), 0.2, 1.0, ((0, 2),), jnp.float32),
    }


@jax.custom_vjp
def low(v):
    return lax.optimization_barrier(v.astype(jnp.bfloat16)).astype(jnp.float32)

@jax.custom_vjp
def low_back(v):
    return v

def low_keep(v):
    return (low(v), None)

def low_pass(kept, grad):
    return (grad,)

def back_keep(v):
    return (v, None)

def back_low(kept, grad):
    return (low(grad),)
low.defvjp(low_keep, low_pass)
low_back.defvjp(back_keep, back_low)
EPS = 1e-05
QUERY_SCALE = 0.125
HIGHEST = lax.Precision.HIGHEST

def layer_norm(values, gain_vec, bias_vec):
    average = lax.optimization_barrier(jnp.mean(values, -1, keepdims=True))
    centered = values - average
    variance = lax.optimization_barrier(jnp.mean(centered * centered, -1, keepdims=True))
    return centered * lax.rsqrt(variance + EPS) * gain_vec + bias_vec

def project(values, matrix):
    return jnp.einsum('...i,ij->...j', values, matrix, precision=HIGHEST)

def softmax_rows(scores):
    row_max = lax.optimization_barrier(jnp.max(scores, -1, keepdims=True))
    exponent = jnp.exp(scores - row_max)
    return exponent / lax.optimization_barrier(jnp.sum(exponent, -1, keepdims=True))

def resampler_layer(latent_rows, media_rows, params):
    query_matrix, key_matrix, value_matrix, output_matrix, up_matrix, down_matrix, media_gain, media_bias, latent_gain, latent_bias, feed_gain, feed_bias = params
    images = latent_rows.shape[0]
    latent_count = latent_rows.shape[1]
    key_count = latent_count + media_rows.shape[1]
    heads_count = query_matrix.shape[1] // DH
    normed_media = low(layer_norm(media_rows, media_gain, media_bias))
    normed_latent = low(layer_norm(latent_rows, latent_gain, latent_bias))
    queries = low_back(low(project(normed_latent, query_matrix) * QUERY_SCALE))
    kv_input = jnp.concatenate([normed_media, normed_latent], axis=1)
    key_rows = low_back(low(project(kv_input, key_matrix)))
    value_rows = low_back(low(project(kv_input, value_matrix)))
    query_heads = queries.reshape(images, latent_count, heads_count, DH)
    key_heads = key_rows.reshape(images, key_count, heads_count, DH)
    value_heads = value_rows.reshape(images, key_count, heads_count, DH)
    scores = low_back(jnp.einsum('blhd,bkhd->bhlk', query_heads, key_heads, precision=HIGHEST))
    probs_low = low(softmax_rows(scores))
    attended = jnp.einsum('bhlk,bkhd->blhd', probs_low, value_heads, precision=HIGHEST)
    attended = low_back(low(attended.reshape(images, latent_count, heads_count * DH)))
    after_attn = latent_rows + low_back(project(attended, output_matrix))
    normed_feed = low(layer_norm(after_attn, feed_gain, feed_bias))
    hidden = low_back(project(normed_feed, up_matrix))
    activated = low(jax.nn.gelu(hidden, approximate=False))
    return after_attn + low_back(project(activated, down_matrix))

def reference(latents, media_tokens, image_counts, cotangent, query_weight, key_weight, value_weight, output_weight, up_weight, down_weight, media_gain, media_bias, latent_gain, latent_bias, feed_gain, feed_bias):
    slot_mask = (jnp.arange(SLOTS)[None, None, :] < image_counts[:, :, None]).astype(jnp.float32)
    weights = (query_weight.astype(jnp.float32), key_weight.astype(jnp.float32), value_weight.astype(jnp.float32), output_weight.astype(jnp.float32), up_weight.astype(jnp.float32), down_weight.astype(jnp.float32), media_gain.astype(jnp.float32), media_bias.astype(jnp.float32), latent_gain.astype(jnp.float32), latent_bias.astype(jnp.float32), feed_gain.astype(jnp.float32), feed_bias.astype(jnp.float32))

    def forward(latent_in, media_in, params):
        groups = MB * SAMPLES
        latent_groups = latent_in.reshape(groups, SLOTS, LAT, D)
        media_groups = media_in.reshape(groups, SLOTS, PATCH, D)
        first_layer = tuple((param[0] for param in params))
        second_layer = tuple((param[1] for param in params))

        def one_group(pair_rows):
            latent_block, media_block = pair_rows
            middle = low_back(low(resampler_layer(latent_block, media_block, first_layer)))
            return resampler_layer(middle, media_block, second_layer)
        result = lax.map(jax.checkpoint(one_group), (latent_groups, media_groups))
        return result.reshape(latent_in.shape) * slot_mask[..., None, None]
    resampled, pullback = jax.vjp(forward, latents.astype(jnp.float32), media_tokens.astype(jnp.float32), weights)
    latent_grad, media_grad, weight_grads = pullback(cotangent.astype(jnp.float32))
    return (resampled.astype(jnp.bfloat16), latent_grad, media_grad, weight_grads[0], weight_grads[1], weight_grads[2], weight_grads[3], weight_grads[4], weight_grads[5], weight_grads[6], weight_grads[7], weight_grads[8], weight_grads[9], weight_grads[10], weight_grads[11])
```

```python
import functools

import jax
import jax.numpy as jnp
from jax import lax
from jax.experimental import pallas as pl
from jax.experimental.pallas import tpu as pltpu
from jax.sharding import PartitionSpec as P

DH = 64
EPS = 1e-05
QUERY_SCALE = 0.125
QUAD = 4
GROUP = 2
F32, BF16 = jnp.float32, jnp.bfloat16


def dot(a, b):
    return lax.dot_general(a, b, (((1,), (0,)), ((), ())), preferred_element_type=F32)


def dot_nt(a, b):
    return lax.dot_general(a, b, (((1,), (1,)), ((), ())), preferred_element_type=F32)


def dot_tn(a, b):
    return lax.dot_general(a, b, (((0,), (0,)), ((), ())), preferred_element_type=F32)


def standardize(rows):
    centered = rows - jnp.mean(rows, -1, keepdims=True)
    inverse = lax.rsqrt(jnp.mean(centered * centered, -1, keepdims=True) + EPS)
    return centered * inverse, inverse


def gelu_parts(hidden):
    t = 1.0 / (1.0 + (0.3275911 * 0.5**0.5) * jnp.abs(hidden))
    bell = jnp.exp(hidden * hidden * -0.5)
    series = 0.5 * 1.061405429
    for term in (-1.453152027, 1.421413741, -0.284496736, 0.254829592):
        series = series * t + 0.5 * term
    tail = series * t * bell
    below = jnp.where(hidden < 0.0, tail, 1.0 - tail)
    return hidden * below, below + hidden * bell * 0.3989422804014327


def norm_back(grads, standard, inverse, gain):
    scaled = grads * gain
    return inverse * (
        scaled
        - jnp.mean(scaled, -1, keepdims=True)
        - standard * jnp.mean(scaled * standard, -1, keepdims=True)
    )


def layers_kernel(
    dims,
    counts,
    media_gain,
    media_bias,
    latent_gain,
    latent_bias,
    feed_gain,
    feed_bias,
    latents,
    media,
    cotangent,
    wq_hbm,
    wk_hbm,
    wv_hbm,
    wo_hbm,
    up_hbm,
    down_hbm,
    gg_out,
    dh_out,
    nf_out,
    df_out,
    att_out,
    da_out,
    dq_out,
    kin_out,
    dkv_out,
    rows_out,
    latgrad_out,
    dmed_out,
    norm_grads,
    wq,
    wkv,
    wo,
    up,
    down,
    med_in,
    x_in,
    g_in,
    q_keep,
    kv_keep,
    pr_keep,
    x1_keep,
    slope_keep,
    y_stage,
    dy_stage,
    kin_st,
    dkv_st,
    gg_st,
    dh_st,
    nf_st,
    df_st,
    att_st,
    da_st,
    dq_st,
    dmed_st,
    acc,
    dkin,
    w_sem,
    own_sem,
    xown_sem,
    gown_sem,
    med_send,
    med_recv,
    x_send,
    x_recv,
    g_send,
    g_recv,
    f_sem,
    b_sem,
    row_sem,
    lg_sem,
):
    chunks, patches, lat, d, inner, ff, slots = dims
    keys = patches + lat
    rows = GROUP * lat
    half = d // 2
    quads = inner // (QUAD * DH)
    qw = QUAD * DH
    sec = lax.axis_index("section")
    peer = 1 - sec
    first = sec == 0
    mine = pl.ds(pl.multiple_of(sec * half, half), half)
    theirs = pl.ds(pl.multiple_of(peer * half, half), half)
    there = {"section": peer}

    def remote(src, dst, send, recv):
        return pltpu.make_async_remote_copy(
            src_ref=src,
            dst_ref=dst,
            send_sem=send,
            recv_sem=recv,
            device_id=there,
            device_id_type=pl.DeviceIdType.MESH,
        )

    def group(c):
        return pl.ds(c * GROUP, GROUP)

    images = chunks * GROUP

    def med_copy(n):
        return remote(
            media.at[n], med_in.at[n, :, mine], med_send.at[n], med_recv.at[n]
        )

    def med_arrival(n):
        return remote(
            media.at[n], med_in.at[n, :, theirs], med_send.at[n], med_recv.at[n]
        )

    def half_copy(src, dst, send, recv, c, where):
        return remote(src.at[group(c)], dst.at[group(c), :, where], send.at[c], recv.at[c])

    def whole_copy(src, dst, send, recv, c):
        return remote(src.at[group(c)], dst.at[group(c)], send.at[c], recv.at[c])

    def med_own(c):
        return pltpu.make_async_copy(
            media.at[group(c)], med_in.at[group(c), :, mine], own_sem.at[c]
        )

    lat_own = pltpu.make_async_copy(latents, x_in.at[:, :, mine], xown_sem)
    cot_own = pltpu.make_async_copy(cotangent, g_in.at[:, :, mine], gown_sem)

    weight_copies = [
        pltpu.make_async_copy(wk_hbm, wkv.at[:, pl.ds(0, inner)], w_sem.at[0]),
        pltpu.make_async_copy(wv_hbm, wkv.at[:, pl.ds(inner, inner)], w_sem.at[1]),
        pltpu.make_async_copy(wq_hbm, wq, w_sem.at[2]),
        pltpu.make_async_copy(wo_hbm, wo, w_sem.at[3]),
        pltpu.make_async_copy(up_hbm, up, w_sem.at[4]),
        pltpu.make_async_copy(down_hbm, down, w_sem.at[5]),
    ]

    barrier = pltpu.get_barrier_semaphore()
    pl.semaphore_signal(
        barrier, inc=1, device_id=there, device_id_type=pl.DeviceIdType.MESH
    )
    pl.semaphore_wait(barrier, 1)

    for c in range(chunks):
        med_own(c).start()

    @pl.when(first)
    def _():
        lat_own.start()
        for n in range(GROUP):
            med_copy(n).start()
        half_copy(cotangent, g_in, g_send, g_recv, 0, mine).start()

    @pl.when(jnp.logical_not(first))
    def _():
        cot_own.start()
        half_copy(latents, x_in, x_send, x_recv, 0, mine).start()
        for n in range(GROUP):
            med_copy(n).start()

    for copy in weight_copies:
        copy.start()
    norm_grads[...] = jnp.zeros_like(norm_grads)

    early = min(2 * GROUP, images)

    @pl.when(first)
    def _():
        lat_own.wait()
        for n in range(GROUP, early):
            med_copy(n - GROUP).wait_send()
            med_copy(n).start()

    @pl.when(jnp.logical_not(first))
    def _():
        cot_own.wait()
        for n in range(GROUP, early):
            med_copy(n - GROUP).wait_send()
            if n % GROUP == 0:
                half_copy(latents, x_in, x_send, x_recv, n // GROUP, mine).start()
            med_copy(n).start()

    def lane_head(n, h):
        return (lax.broadcasted_iota(jnp.int32, (n, qw), 1) // DH) == h

    def spread(quad_rows):
        return jnp.concatenate(
            [
                jnp.where(lane_head(lat, h), quad_rows, jnp.zeros_like(quad_rows))
                for h in range(QUAD)
            ],
            axis=0,
        )

    def gather_heads(stacked):
        total = jnp.where(lane_head(lat, 0), stacked[:lat], 0.0)
        for h in range(1, QUAD):
            total = total + jnp.where(
                lane_head(lat, h), stacked[h * lat : (h + 1) * lat], 0.0
            )
        return total

    def f_copies(c):
        r = pl.ds(c * rows, rows)
        return [
            pltpu.make_async_copy(gg_st, gg_out.at[:, r], f_sem.at[0]),
            pltpu.make_async_copy(nf_st, nf_out.at[r], f_sem.at[1]),
            pltpu.make_async_copy(att_st, att_out.at[r], f_sem.at[2]),
            pltpu.make_async_copy(
                kin_st, kin_out.at[pl.ds(c * GROUP * keys, GROUP * keys)], f_sem.at[3]
            ),
        ]

    def b_copies(c):
        r = pl.ds(c * rows, rows)
        return [
            pltpu.make_async_copy(dh_st, dh_out.at[:, r], b_sem.at[0]),
            pltpu.make_async_copy(df_st, df_out.at[r], b_sem.at[1]),
            pltpu.make_async_copy(da_st, da_out.at[r], b_sem.at[2]),
            pltpu.make_async_copy(dq_st, dq_out.at[r], b_sem.at[3]),
            pltpu.make_async_copy(
                dkv_st, dkv_out.at[pl.ds(c * GROUP * keys, GROUP * keys)], b_sem.at[4]
            ),
            pltpu.make_async_copy(dmed_st.at[0], dmed_out.at[0, group(c)], b_sem.at[5]),
            pltpu.make_async_copy(dmed_st.at[1], dmed_out.at[1, group(c)], b_sem.at[6]),
        ]

    def row_copy(c):
        return pltpu.make_async_copy(
            y_stage.at[group(c)], rows_out.at[group(c)], row_sem.at[c]
        )

    def lg_copy(c):
        return pltpu.make_async_copy(
            dy_stage.at[group(c)], latgrad_out.at[group(c)], lg_sem.at[c]
        )

    def mask_of(image):
        sample = image // slots
        return jnp.where(image - sample * slots < counts[sample], 1.0, 0.0)

    step_rows = 64
    ff_tile = d // 2

    def forward(c):
        @pl.when(c > 0)
        def _():
            for copy in f_copies(c - 1):
                copy.wait()

        med_own(c).wait()
        for i in range(GROUP):
            med_arrival(c * GROUP + i).wait_recv()

        for i in range(GROUP):

            def media_rows(k, carry, i=i):
                r = pl.ds(pl.multiple_of(k * step_rows, step_rows), step_rows)
                standard, _ = standardize(med_in[c * GROUP + i, r, :].astype(F32))
                to = pl.ds(pl.multiple_of(i * keys + k * step_rows, step_rows), step_rows)
                kin_st[to, :] = (standard * media_gain[...] + media_bias[...]).astype(BF16)
                return carry

            lax.fori_loop(0, patches // step_rows, media_rows, 0, unroll=True)

        @pl.when(first)
        def _():
            half_copy(latents, x_in, x_send, x_recv, c, theirs).wait_recv()

        @pl.when(jnp.logical_not(first))
        def _():
            whole_copy(y_stage, x_in, x_send, x_recv, c).wait_recv()

        for i in range(GROUP):
            standard, _ = standardize(x_in[c * GROUP + i].astype(F32))
            kin_st[i * keys + patches : (i + 1) * keys, :] = (
                standard * latent_gain[...] + latent_bias[...]
            ).astype(BF16)

        @pl.when(c == 0)
        def _():
            for copy in weight_copies[:4]:
                copy.wait()

        n_tile = 256

        def kv_tile(j, carry):
            cols = pl.ds(pl.multiple_of(j * n_tile, n_tile), n_tile)
            kv_keep[c, :, cols] = dot(kin_st[...], wkv[:, cols]).astype(BF16)
            return carry

        lax.fori_loop(0, 2 * inner // n_tile, kv_tile, 0)
        nx = jnp.concatenate(
            [kin_st[i * keys + patches : (i + 1) * keys, :] for i in range(GROUP)], axis=0
        )
        q_keep[c] = (dot(nx, wq[...]) * QUERY_SCALE).astype(BF16)

        for i in range(GROUP):
            for g in range(quads):
                lanes = slice(g * qw, (g + 1) * qw)
                r = slice(i * keys, (i + 1) * keys)
                stack = spread(q_keep[c, i * lat : (i + 1) * lat, lanes])
                scores = dot_nt(stack, kv_keep[c, r, lanes])
                top = jnp.max(scores, -1, keepdims=True)
                powers = jnp.exp(scores - top)
                probs = (powers * (1.0 / jnp.sum(powers, -1, keepdims=True))).astype(BF16)
                pr_keep[c, i * quads + g] = probs
                mixed = dot(probs, kv_keep[c, r, inner + g * qw : inner + (g + 1) * qw])
                att_st[i * lat : (i + 1) * lat, lanes] = gather_heads(mixed).astype(BF16)

        x1 = x_in[group(c)].reshape(rows, d).astype(F32) + dot(att_st[...], wo[...])
        x1_keep[c] = x1
        standard, _ = standardize(x1)
        nf_st[...] = (standard * feed_gain[...] + feed_bias[...]).astype(BF16)

        @pl.when(c == 0)
        def _():
            for copy in weight_copies[4:]:
                copy.wait()

        acc[...] = x1

        tiles = ff // ff_tile
        normed = nf_st[...]
        hidden = dot(normed, up[:, :ff_tile])
        for j in range(tiles):
            if j + 1 < tiles:
                ahead = dot(normed, up[:, (j + 1) * ff_tile : (j + 2) * ff_tile])
            active, slope = gelu_parts(hidden)
            slope_keep[c, :, j * ff_tile : (j + 1) * ff_tile] = slope.astype(BF16)
            active = active.astype(BF16)
            gg_st[j] = active
            acc[...] += dot(active, down[j * ff_tile : (j + 1) * ff_tile, :])
            hidden = ahead

        for i in range(GROUP):
            scale = jnp.where(first, 1.0, mask_of(c * GROUP + i))
            y_stage[c * GROUP + i] = (acc[i * lat : (i + 1) * lat, :] * scale).astype(BF16)

        @pl.when(first)
        def _():
            whole_copy(y_stage, x_in, x_send, x_recv, c).start()

            @pl.when(c + 2 < chunks)
            def _():
                for i in range(GROUP):
                    med_copy((c + 2) * GROUP + i).start()

            @pl.when(c + 1 < chunks)
            def _():
                half_copy(cotangent, g_in, g_send, g_recv, c + 1, mine).start()

        @pl.when(jnp.logical_not(first))
        def _():
            row_copy(c).start()

        for copy in f_copies(c):
            copy.start()

    def backward(c):
        @pl.when(c > 0)
        def _():
            for copy in b_copies(c - 1):
                copy.wait()

        @pl.when(first)
        def _():
            whole_copy(dy_stage, g_in, g_send, g_recv, c).wait_recv()

        @pl.when(jnp.logical_not(first))
        def _():
            half_copy(cotangent, g_in, g_send, g_recv, c, theirs).wait_recv()

        for i in range(GROUP):
            scale = jnp.where(first, 1.0, mask_of(c * GROUP + i))
            df_st[i * lat : (i + 1) * lat, :] = (
                g_in[c * GROUP + i].astype(F32) * scale
            ).astype(BF16)
        tiles = ff // ff_tile
        grads_low = df_st[...]
        dg = dot_nt(grads_low, down[:ff_tile, :])
        for j in range(tiles):
            if j + 1 < tiles:
                ahead = dot_nt(grads_low, down[(j + 1) * ff_tile : (j + 2) * ff_tile, :])
            slope = slope_keep[c, :, j * ff_tile : (j + 1) * ff_tile].astype(F32)
            dh = (dg * slope).astype(BF16)
            dh_st[j] = dh
            more = dot_nt(dh, up[:, j * ff_tile : (j + 1) * ff_tile])
            acc[...] = more if j == 0 else acc[...] + more
            dg = ahead
        standard, inverse = standardize(x1_keep[c])
        dnf = acc[...]
        norm_grads[4:5, :] += jnp.sum(dnf * standard, axis=0, keepdims=True)
        norm_grads[5:6, :] += jnp.sum(dnf, axis=0, keepdims=True)
        dx1 = df_st[...].astype(F32) + norm_back(dnf, standard, inverse, feed_gain[...])
        acc[...] = dx1
        da_st[...] = dx1.astype(BF16)
        datt = dot_nt(da_st[...], wo[...]).astype(BF16)
        for i in range(GROUP):
            for g in range(quads):
                lanes = slice(g * qw, (g + 1) * qw)
                vlanes = slice(inner + g * qw, inner + (g + 1) * qw)
                r = slice(i * keys, (i + 1) * keys)
                lr = slice(i * lat, (i + 1) * lat)
                stack = spread(datt[lr, lanes])
                dp = dot_nt(stack, kv_keep[c, r, vlanes])
                probs = pr_keep[c, i * quads + g]
                dkv_st[r, vlanes] = dot_tn(probs, stack).astype(BF16)
                wide = probs.astype(F32)
                ds = (wide * (dp - jnp.sum(wide * dp, -1, keepdims=True))).astype(BF16)
                dkv_st[r, lanes] = dot_tn(ds, spread(q_keep[c, lr, lanes])).astype(BF16)
                mixed = gather_heads(dot(ds, kv_keep[c, r, lanes])).astype(BF16)
                dq_st[lr, lanes] = (mixed.astype(F32) * QUERY_SCALE).astype(BF16)

        d_lat = jnp.concatenate(
            [dkv_st[i * keys + patches : (i + 1) * keys, :] for i in range(GROUP)], axis=0
        )
        dnx = dot_nt(d_lat, wkv[...]) + dot_nt(dq_st[...], wq[...])
        standard, inverse = standardize(x_in[group(c)].reshape(rows, d).astype(F32))
        norm_grads[2:3, :] += jnp.sum(dnx * standard, axis=0, keepdims=True)
        norm_grads[3:4, :] += jnp.sum(dnx, axis=0, keepdims=True)
        dx = acc[...] + norm_back(dnx, standard, inverse, latent_gain[...])
        dy_stage[group(c)] = dx.astype(BF16).reshape(GROUP, lat, d)

        @pl.when(first)
        def _():
            lg_copy(c).start()

        @pl.when(jnp.logical_not(first))
        def _():
            whole_copy(dy_stage, g_in, g_send, g_recv, c).start()

        for i in range(GROUP):
            dkin[...] = dot_nt(dkv_st[i * keys : i * keys + patches, :], wkv[...])

            def media_rows(k, carry, i=i):
                r = pl.ds(pl.multiple_of(k * step_rows, step_rows), step_rows)
                standard, inverse = standardize(med_in[c * GROUP + i, r, :].astype(F32))
                grads = dkin[r, :]
                norm_grads[0:1, :] += jnp.sum(grads * standard, axis=0, keepdims=True)
                norm_grads[1:2, :] += jnp.sum(grads, axis=0, keepdims=True)
                out = norm_back(grads, standard, inverse, media_gain[...]).astype(BF16)
                dmed_st[0, i, r, :] = out[:, :half]
                dmed_st[1, i, r, :] = out[:, half:]
                return carry

            lax.fori_loop(0, patches // step_rows, media_rows, 0, unroll=True)

        for copy in b_copies(c):
            copy.start()

    def step(t, carry):
        second = t // 2
        is_forward = jnp.where(first, t < chunks, t - second * 2 == 0)

        @pl.when(jnp.logical_not(first) & (t + 2 < chunks))
        def _():
            half_copy(latents, x_in, x_send, x_recv, t + 2, mine).start()
            for i in range(GROUP):
                med_copy((t + 2) * GROUP + i).start()

        c = jnp.where(first, jnp.where(t < chunks, t, t - chunks), second)

        @pl.when(is_forward)
        def _():
            forward(c)

        @pl.when(jnp.logical_not(is_forward))
        def _():
            backward(c)

        return carry

    lax.fori_loop(0, 2 * chunks, step, 0)

    for copy in f_copies(chunks - 1) + b_copies(chunks - 1):
        copy.wait()

    @pl.when(first)
    def _():
        for n in range(early - GROUP, images):
            med_copy(n).wait_send()
        for c in range(chunks):
            lg_copy(c).wait()
            whole_copy(y_stage, x_in, x_send, x_recv, c).wait_send()
            half_copy(cotangent, g_in, g_send, g_recv, c, mine).wait_send()

    @pl.when(jnp.logical_not(first))
    def _():
        for n in range(early - GROUP, images):
            med_copy(n).wait_send()
        for c in range(chunks):
            row_copy(c).wait()
            half_copy(latents, x_in, x_send, x_recv, c, mine).wait_send()
            whole_copy(dy_stage, g_in, g_send, g_recv, c).wait_send()


def run_layers(latents, media, cotangent, counts, weights, norms, slots):
    images, lat, half = latents.shape
    patches = media.shape[1]
    d = 2 * half
    wq, wk, wv, wo, up, down = weights
    inner, ff = wq.shape[1], up.shape[1]
    chunks = images // GROUP
    keys = patches + lat
    rows = GROUP * lat
    quads = inner // (QUAD * DH)
    dims = (chunks, patches, lat, d, inner, ff, slots)
    total, wide = images * lat, images * keys

    def out(*shape, dtype=BF16):
        return jax.ShapeDtypeStruct(shape, dtype)

    any_spec = pl.BlockSpec(memory_space=pl.ANY)
    vmem_spec = pl.BlockSpec(memory_space=pltpu.VMEM)
    dma = pltpu.SemaphoreType.DMA
    return pl.pallas_call(
        functools.partial(layers_kernel, dims),
        out_shape=(
            out(2 * ff // d, total, half),
            out(2 * ff // d, total, half),
            out(total, d),
            out(total, d),
            out(total, inner),
            out(total, d),
            out(total, inner),
            out(wide, d),
            out(wide, 2 * inner),
            out(images, lat, d),
            out(images, lat, d),
            out(2, images, patches, half),
            out(8, d, dtype=F32),
        ),
        in_specs=[pl.BlockSpec(memory_space=pltpu.SMEM)] + [vmem_spec] * 6 + [any_spec] * 9,
        out_specs=(any_spec,) * 12 + (vmem_spec,),
        scratch_shapes=[
            pltpu.VMEM((d, inner), BF16),
            pltpu.VMEM((d, 2 * inner), BF16),
            pltpu.VMEM((inner, d), BF16),
            pltpu.VMEM((d, ff), BF16),
            pltpu.VMEM((ff, d), BF16),
            pltpu.VMEM((images, patches, d), BF16),
            pltpu.VMEM((images, lat, d), BF16),
            pltpu.VMEM((images, lat, d), BF16),
            pltpu.VMEM((chunks, rows, inner), BF16),
            pltpu.VMEM((chunks, GROUP * keys, 2 * inner), BF16),
            pltpu.VMEM((chunks, GROUP * quads, QUAD * lat, keys), BF16),
            pltpu.VMEM((chunks, rows, d), F32),
            pltpu.VMEM((chunks, rows, ff), BF16),
            pltpu.VMEM((images, lat, d), BF16),
            pltpu.VMEM((images, lat, d), BF16),
            pltpu.VMEM((GROUP * keys, d), BF16),
            pltpu.VMEM((GROUP * keys, 2 * inner), BF16),
            pltpu.VMEM((2 * ff // d, rows, half), BF16),
            pltpu.VMEM((2 * ff // d, rows, half), BF16),
            pltpu.VMEM((rows, d), BF16),
            pltpu.VMEM((rows, d), BF16),
            pltpu.VMEM((rows, inner), BF16),
            pltpu.VMEM((rows, d), BF16),
            pltpu.VMEM((rows, inner), BF16),
            pltpu.VMEM((2, GROUP, patches, half), BF16),
            pltpu.VMEM((rows, d), F32),
            pltpu.VMEM((patches, d), F32),
            dma((6,)),
            dma((chunks,)),
            dma,
            dma,
            dma((images,)),
            dma((images,)),
            dma((chunks,)),
            dma((chunks,)),
            dma((chunks,)),
            dma((chunks,)),
            dma((4,)),
            dma((7,)),
            dma((chunks,)),
            dma((chunks,)),
        ],
        compiler_params=pltpu.CompilerParams(
            collective_id=0, has_side_effects=True, vmem_limit_bytes=63 * 2**20
        ),
        cost_estimate=pl.CostEstimate(
            flops=4 * images * 960_000_000, bytes_accessed=80_000_000, transcendentals=0
        ),
        name="layers",
    )(counts, *norms, latents, media, cotangent, wq, wk, wv, wo, up, down)


def reduce_kernel(
    dims,
    norm_grads,
    gg,
    dh,
    nf,
    df,
    att,
    da,
    dq,
    kin,
    dkv,
    rows_in,
    latgrad,
    dmed,
    main_out,
    attn_out,
    came,
    med_came,
    g_up1,
    g_up0,
    g_down0,
    g_low,
    g_high,
    g_attn,
    core_slots,
    x_up1,
    x_up0,
    x_down0,
    x_low,
    x_high,
    x_attn,
    z_up1,
    z_up0,
    z_down0,
    z_low,
    z_high,
    z_attn,
    buf_a,
    buf_b,
    flipped,
    att_v,
    dq_v,
    big_a,
    dh_v,
    big_b,
    stage,
    attn_stage,
    load_sem,
    core_send,
    core_recv,
    x_send,
    x_recv,
    zr_send,
    zr_recv,
    zl_send,
    zl_recv,
    y_send,
    y_recv,
    credit,
    main_sem,
    attn_sem,
):
    images, lat, patches, d, inner, ff, dp = dims
    line = dp // 4
    keys = lat + patches
    total = images * lat
    block = ff // dp // 2
    half = d // 2
    blocks = ff // half
    me = lax.axis_index("dp")
    sec = lax.axis_index("section")
    z = me // 4
    x = me // 2 - z * 2
    c = me - (me // 2) * 2
    sibling = {"dp": me + 1 - 2 * c}
    across = {"dp": me + 2 - 4 * x}
    ahead = {"dp": jnp.minimum(me + 4, dp - 4 + (me - z * 4))}
    behind = {"dp": jnp.maximum(me - 4, me - z * 4)}
    peer = {"section": 1 - sec}
    has_left, has_right = z > 0, z < line - 1
    mesh_ids = pl.DeviceIdType.MESH

    def place(dest):
        return dest % 2, (dest // 2) % 2, dest // 4

    def remote(src, dst, send, recv, device):
        return pltpu.make_async_remote_copy(
            src_ref=src,
            dst_ref=dst,
            send_sem=send,
            recv_sem=recv,
            device_id=device,
            device_id_type=mesh_ids,
        )

    barrier = pltpu.get_barrier_semaphore()
    for device in (sibling, across, peer):
        pl.semaphore_signal(barrier, inc=1, device_id=device, device_id_type=mesh_ids)

    @pl.when(has_left)
    def _():
        pl.semaphore_signal(barrier, inc=1, device_id=behind, device_id_type=mesh_ids)

    @pl.when(has_right)
    def _():
        pl.semaphore_signal(barrier, inc=1, device_id=ahead, device_id_type=mesh_ids)

    def load(src, dst, k):
        return pltpu.make_async_copy(src, dst, load_sem.at[k])

    part = pl.ds(0, images * keys)
    loads = {
        "nf": load(nf, buf_a, 0),
        "dh": load(dh, dh_v, 1),
        "df": load(df, buf_b, 2),
        "gg": load(gg, big_b, 3),
        "att": load(att, att_v, 4),
        "dq": load(dq, dq_v, 5),
        "da": load(da, buf_a, 6),
        "kin": load(kin, big_a, 7),
        "dk": load(dkv.at[:, pl.ds(0, inner)], big_b.at[part], 8),
        "dv": load(dkv.at[:, pl.ds(inner, inner)], big_b.at[part], 9 + images),
    }
    nx_loads = [
        load(kin.at[pl.ds(i * keys + patches, lat)], buf_b.at[pl.ds(i * lat, lat)], 9 + i)
        for i in range(images)
    ]
    for name in ("nf", "dh", "df", "gg", "att", "dq", "kin"):
        loads[name].start()

    pl.semaphore_wait(
        barrier, 3 + jnp.where(has_left, 1, 0) + jnp.where(has_right, 1, 0)
    )

    def out_rows(src, lanes):
        return remote(src.at[:, :, lanes], came, y_send.at[0], y_recv.at[0], peer)

    out_first = out_rows(latgrad, pl.ds(half, half))
    out_second = out_rows(rows_in, pl.ds(0, half))
    out_media = remote(dmed.at[1 - sec], med_came, y_send.at[1], y_recv.at[1], peer)

    @pl.when(sec == 0)
    def _():
        out_first.start()

    @pl.when(sec == 1)
    def _():
        out_second.start()

    out_media.start()

    grads = [g_up1, g_up0, g_down0, g_low, g_high, g_attn]
    count = len(grads)
    core_in = [
        core_slots.at[n % 2, :, :, pl.ds(0, grads[n].shape[3])] for n in range(count)
    ]
    x_in = [x_up1, x_up0, x_down0, x_low, x_high, x_attn]
    z_in = [z_up1, z_up0, z_down0, z_low, z_high, z_attn]
    z_first = 0

    def up_piece(h):
        wide = ff // dp
        groups = half // block
        for j in range(blocks):
            tile = dot(
                flipped[h * half : (h + 1) * half, :], dh_v[j * total : (j + 1) * total, :]
            ).astype(BF16)
            for i in range(half // wide):
                pc, px, pz = place(j * (half // wide) + i)
                for k in range(groups):
                    grads[1 - h][pc, px, pz, :, k * wide : (k + 1) * wide] = tile[
                        k * block : (k + 1) * block, i * wide : (i + 1) * wide
                    ]

    def down_piece(p):
        own = d // dp
        tiles = range(blocks // 2) if p == 2 else range(blocks // 4)
        start = 0 if p == 2 else (p - 1) * (blocks // 4)
        for k in tiles:
            j = start + k
            at = k * half
            r = slice(at // d * own, at // d * own + own)
            lanes = slice(at % d, at % d + half)
            for m in range(2):
                tile = dot(
                    flipped[m * half : (m + 1) * half, :], big_b[j * total : (j + 1) * total, :]
                ).astype(BF16)
                for i in range(half // own):
                    pc, px, pz = place(m * (half // own) + i)
                    grads[p][pc, px, pz, r, lanes] = tile[i * own : (i + 1) * own, :]

    def attn_piece():
        own = inner // dp
        lo = inner // 2

        def store(n, make):
            for m in range(2):
                tile = make(slice(m * lo, (m + 1) * lo)).astype(BF16)
                for i in range(lo // own):
                    pc, px, pz = place(m * (lo // own) + i)
                    g_attn[pc, px, pz, n * own : (n + 1) * own, :] = tile[
                        i * own : (i + 1) * own, :
                    ]

        for copy in nx_loads:
            copy.wait()
        store(0, lambda m: dot_tn(dq_v[:, m], buf_b[...]))
        loads["kin"].wait()
        loads["dk"].wait()
        store(1, lambda m: dot_tn(big_b[: images * keys, m], big_a[...]))
        loads["dv"].start()
        loads["dv"].wait()
        store(2, lambda m: dot_tn(big_b[: images * keys, m], big_a[...]))
        loads["da"].wait()
        out_own = d // dp
        for m in range(2):
            tile = dot_tn(buf_a[:, m * half : (m + 1) * half], att_v[...]).astype(BF16)
            for i in range(half // out_own):
                pc, px, pz = place(m * (half // out_own) + i)
                rest = tile[i * out_own : (i + 1) * out_own, :]
                g_attn[pc, px, pz, 3 * own : 4 * own, :inner] = rest[:own]
                g_attn[pc, px, pz, 3 * own : 4 * own, inner:] = rest[own:]
        lanes = 128
        for dest in range(dp):
            pc, px, pz = place(dest)
            at = (dest * (d // dp)) // lanes * lanes
            sums = norm_grads[:, at : at + lanes]
            g_attn[pc, px, pz, 4 * own :, :] = jnp.zeros((16, d), BF16)
            g_attn[pc, px, pz, 4 * own :, :lanes] = jnp.concatenate(
                [sums, jnp.zeros_like(sums)], axis=0
            ).astype(BF16)

    def core_copy(p):
        return remote(grads[p].at[1 - c], core_in[p], core_send.at[p], core_recv.at[p], sibling)

    def x_copy(p):
        if p == z_first:
            src = grads[p].at[c, 1 - x, z]
        else:
            src = grads[p].at[c, 1 - x]
        return remote(src, x_in[p], x_send.at[p], x_recv.at[p], across)

    def spot(p, t):
        if p == z_first:
            return grads[p].at[c, :, t]
        return grads[p].at[c, x, t]

    def right_copy(p, t):
        k = p * line + t
        return remote(spot(p, t), z_in[p].at[t + 1], zr_send.at[k], zr_recv.at[k], ahead)

    def left_copy(p, t):
        k = p * line + t
        return remote(spot(p, t), z_in[p].at[t], zl_send.at[k], zl_recv.at[k], behind)

    def add_into(target, source):
        target[...] = (target[...].astype(F32) + source[...].astype(F32)).astype(BF16)

    def core_add(p):
        core_copy(p).wait_recv()

        def body(n, carry):
            xx = n // line
            zz = n - xx * line
            add_into(grads[p].at[c, xx, zz], core_in[p].at[xx, zz])
            return carry

        lax.fori_loop(0, 2 * line, body, 0)

    def x_add(p):
        x_copy(p).wait_recv()

        def body(zz, carry):
            add_into(grads[p].at[c, x, zz], x_in[p].at[zz])
            return carry

        lax.fori_loop(0, line, body, 0)

    def z_ends(p):
        @pl.when(z == 0)
        def _():
            for t in range(line - 1, 0, -1):
                right_copy(p, t).start()

        @pl.when(z == line - 1)
        def _():
            for t in range(line - 1):
                left_copy(p, t).start()

    def z_phase(p, k):
        t = line - 1 - k

        @pl.when(has_left & (z < t))
        def _():
            right_copy(p, t).wait_recv()
            add_into(spot(p, t), z_in[p].at[t + 1])
            right_copy(p, t).start()

        @pl.when(has_right & (z > k))
        def _():
            left_copy(p, k).wait_recv()
            add_into(spot(p, k), z_in[p].at[k])
            left_copy(p, k).start()

    def z_own(p):
        @pl.when(has_left)
        def _():
            for t in range(1, line):

                @pl.when(z == t)
                def _():
                    right_copy(p, t).wait_recv()
                    add_into(spot(p, t), z_in[p].at[t + 1])

        @pl.when(has_right)
        def _():
            for t in range(line - 1):

                @pl.when(z == t)
                def _():
                    left_copy(p, t).wait_recv()
                    add_into(spot(p, t), z_in[p].at[t])

    rows_of = [(block, block), (0, block), (2 * block, block), (3 * block, block // 2)]
    rows_of.append((3 * block + block // 2, block // 2))

    def main_copy(p):
        at, tall = rows_of[p]
        return pltpu.make_async_copy(
            stage.at[pl.ds(0, tall)], main_out.at[pl.ds(at, tall)], main_sem.at[p]
        )

    attn_copy = pltpu.make_async_copy(attn_stage, attn_out, attn_sem)
    staged = []

    def finish(p):
        result = grads[p].at[c, x, z][...].astype(F32)
        if p == z_first:
            result = result + x_in[p][...].astype(F32)
        if p == count - 1:
            attn_stage[...] = result
            attn_copy.start()
        else:
            if staged:
                main_copy(staged.pop()).wait()
            stage[: rows_of[p][1], :] = result
            main_copy(p).start()
            staged.append(p)

    def give_credit():
        pl.semaphore_signal(credit, inc=1, device_id=sibling, device_id_type=mesh_ids)

    loads["nf"].wait()
    flipped[...] = buf_a[...].T
    loads["da"].start()
    loads["dh"].wait()
    up_piece(1)
    core_copy(0).start()
    up_piece(0)
    core_copy(1).start()
    core_add(0)
    give_credit()
    z_ends(0)
    loads["df"].wait()
    flipped[...] = buf_b[...].T
    for copy in nx_loads:
        copy.start()
    loads["gg"].wait()
    core_add(1)
    give_credit()
    x_copy(1).start()
    down_piece(2)
    pl.semaphore_wait(credit, 1)
    core_copy(2).start()
    down_piece(3)
    pl.semaphore_wait(credit, 1)
    core_copy(3).start()
    core_add(2)
    give_credit()
    x_copy(2).start()
    z_phase(0, 0)
    down_piece(4)
    pl.semaphore_wait(credit, 1)
    core_copy(4).start()
    loads["dk"].start()
    core_add(3)
    give_credit()
    for k in range(1, line - 1):
        z_phase(0, k)
    loads["att"].wait()
    loads["dq"].wait()
    attn_piece()
    pl.semaphore_wait(credit, 1)
    core_copy(5).start()
    core_add(4)
    z_own(0)
    x_copy(0).start()
    core_add(5)
    order = [1, 2, 5, 3, 4]
    for n, p in enumerate(order):
        x_add(p)
        if n + 2 < len(order):
            x_copy(order[n + 2]).start()
        z_ends(p)
        if n > 0:
            z_own(order[n - 1])
            finish(order[n - 1])
        for k in range(line - 1):
            z_phase(p, k)
        if n == 1:
            x_copy(0).wait_recv()
            finish(0)
    z_own(order[-1])
    finish(order[-1])
    main_copy(staged.pop()).wait()
    attn_copy.wait()

    for p in range(count):
        core_copy(p).wait_send()
        x_copy(p).wait_send()
        for t in range(1, line):

            @pl.when(z < t)
            def _(p=p, t=t):
                right_copy(p, t).wait_send()

        for t in range(line - 1):

            @pl.when(z > t)
            def _(p=p, t=t):
                left_copy(p, t).wait_send()

    @pl.when(sec == 0)
    def _():
        out_first.wait()

    @pl.when(sec == 1)
    def _():
        out_second.wait()

    out_media.wait()


def run_reduce(saved, norm_grads, res, latgrad, dmed, dp):
    gg, dh, nf, df, att, da, dq, kin, dkv = saved
    images, lat, d = res.shape
    patches, half = dmed.shape[2:]
    inner, ff = att.shape[1], gg.shape[0] * half
    line = dp // 4
    block = ff // dp // 2
    tall = 4 * inner // dp + 16
    dims = (images, lat, patches, d, inner, ff, dp)
    total, wide = images * lat, images * (lat + patches)
    any_spec = pl.BlockSpec(memory_space=pl.ANY)
    vmem_spec = pl.BlockSpec(memory_space=pltpu.VMEM)
    dma = pltpu.SemaphoreType.DMA
    heights = (block, block, block, block // 2, block // 2, tall)
    pieces = len(heights)

    def low(*shape):
        return pltpu.VMEM(shape, BF16)

    return pl.pallas_call(
        functools.partial(reduce_kernel, dims),
        out_shape=(
            jax.ShapeDtypeStruct((4 * block, d), F32),
            jax.ShapeDtypeStruct((tall, d), F32),
            jax.ShapeDtypeStruct((images, lat, half), BF16),
            jax.ShapeDtypeStruct((images, patches, half), BF16),
        ),
        in_specs=[vmem_spec] + [any_spec] * 12,
        out_specs=(any_spec,) * 4,
        scratch_shapes=[
            *[low(2, 2, line, n, d) for n in heights],
            low(2, 2, line, tall, d),
            low(block, d),
            *[low(line, n, d) for n in heights[1:]],
            low(line + 1, 2, block, d),
            *[low(line + 1, n, d) for n in heights[1:]],
            low(total, d),
            low(total, d),
            low(d, total),
            low(total, inner),
            low(total, inner),
            low(wide, d),
            low(2 * ff // d * total, half),
            low(2 * ff // d * total, half),
            pltpu.VMEM((block, d), F32),
            pltpu.VMEM((tall, d), F32),
            dma((10 + images,)),
            dma((pieces,)),
            dma((pieces,)),
            dma((pieces,)),
            dma((pieces,)),
            dma((pieces * line,)),
            dma((pieces * line,)),
            dma((pieces * line,)),
            dma((pieces * line,)),
            dma((2,)),
            dma((2,)),
            pltpu.SemaphoreType.REGULAR,
            dma((pieces - 1,)),
            dma,
        ],
        compiler_params=pltpu.CompilerParams(
            collective_id=1, has_side_effects=True, vmem_limit_bytes=63 * 2**20
        ),
        cost_estimate=pl.CostEstimate(
            flops=2 * images * 960_000_000, bytes_accessed=60_000_000, transcendentals=0
        ),
        name="reduce",
    )(
        norm_grads,
        gg.reshape(-1, half),
        dh.reshape(-1, half),
        nf,
        df,
        att,
        da,
        dq,
        kin,
        dkv,
        res,
        latgrad,
        dmed,
    )


def outputs_kernel(
    dims,
    where,
    media_own,
    media_came,
    rows_in,
    latgrad,
    came,
    main,
    attn,
    resampled,
    latent_grad,
    media_grad,
    up_out,
    down_out,
    query_out,
    key_out,
    value_out,
    output_out,
    *norm_outs,
):
    block, share, own, inner, d, ff, dp = dims
    first = where[0] == 0
    media_grad[...] = media_own[0].astype(F32) + media_came[...].astype(F32)
    resampled[...] = jnp.where(first, came[...], rows_in[...])
    latent_grad[...] = jnp.where(first, latgrad[...], came[...]).astype(F32)

    @pl.when(pl.program_id(0) == 0)
    def _():
        half, wide = d // 2, ff // dp
        for h in range(2):
            for k in range(half // block):
                at = h * half + k * block
                up_out[at : at + block, :] = main[
                    h * block : (h + 1) * block, k * wide : (k + 1) * wide
                ]
        for k in range(ff // d):
            down_out[:, k * d : (k + 1) * d] = main[
                2 * block + k * share : 2 * block + (k + 1) * share, :
            ]
        query_out[...] = attn[:own, :]
        key_out[...] = attn[own : 2 * own, :]
        value_out[...] = attn[2 * own : 3 * own, :]
        output_out[:own, :] = attn[3 * own : 4 * own, :inner]
        output_out[own:, :] = attn[3 * own : 4 * own, inner:]
        sums = attn[4 * own : 4 * own + 8, :128]
        part = sums[:, :share]
        for n in range(1, 128 // share):
            part = jnp.where(where[1] == n, sums[:, n * share : (n + 1) * share], part)
        for n, out in enumerate(norm_outs):
            out[...] = part[n : n + 1, :]


def run_outputs(dmed, med_came, res, latgrad, came, main, attn, section, dp):
    images, lat, d = res.shape
    patches, half = dmed.shape[2:]
    block = main.shape[0] // 4
    ff = 2 * block * dp
    share = d // dp
    own = (attn.shape[0] - 16) // 4
    inner = own * dp
    place = jnp.stack([section, lax.axis_index("dp") % (128 // share)]).astype(jnp.int32)

    def whole(*shape):
        return pl.BlockSpec(shape, lambda n, w: (0,) * len(shape))

    def part(rows, lanes=0):
        return pl.BlockSpec((1, rows, half), lambda n, w: (n, 0, lanes))

    small = [(d, ff // dp), (share, ff), (own, d), (own, d), (own, d), (share, inner)]
    small += [(1, share)] * 6
    return pl.pallas_call(
        functools.partial(outputs_kernel, (block, share, own, inner, d, ff, dp)),
        out_shape=[
            jax.ShapeDtypeStruct((images, lat, half), BF16),
            jax.ShapeDtypeStruct((images, lat, half), F32),
            jax.ShapeDtypeStruct((images, patches, half), F32),
        ]
        + [jax.ShapeDtypeStruct(shape, F32) for shape in small],
        grid_spec=pltpu.PrefetchScalarGridSpec(
            num_scalar_prefetch=1,
            grid=(images,),
            in_specs=[
                pl.BlockSpec((1, 1, patches, half), lambda n, w: (w[0], n, 0, 0)),
                part(patches),
                part(lat, 1),
                part(lat, 0),
                part(lat),
                whole(*main.shape),
                whole(*attn.shape),
            ],
            out_specs=[part(lat), part(lat), part(patches)] + [whole(*shape) for shape in small],
        ),
        compiler_params=pltpu.CompilerParams(vmem_limit_bytes=62 * 2**20),
        name="outputs",
    )(place, dmed, med_came, res, latgrad, came, main, attn)


def plain_reduce(saved, norm_grads, res, latgrad, dmed, dp):
    gg, dh, nf, df, att, da, dq, kin, dkv = saved
    images, lat, d = res.shape
    patches, half = dmed.shape[2:]
    inner, ff = att.shape[1], gg.shape[0] * half
    section = lax.axis_index("section")
    swap = [(0, 1), (1, 0)]
    to_send = jnp.where(section == 0, latgrad[..., half:], res[..., :half])
    came = lax.ppermute(to_send, "section", swap)
    med_theirs = lax.dynamic_index_in_dim(dmed, 1 - section, 0, keepdims=False)
    med_came = lax.ppermute(med_theirs, "section", swap)
    nx = kin.reshape(images, lat + patches, d)[:, patches:].reshape(images * lat, d)
    gg = gg.swapaxes(0, 1).reshape(images * lat, ff)
    dh = dh.swapaxes(0, 1).reshape(images * lat, ff)
    up_t = dot_tn(dh, nf).astype(BF16).reshape(dp, ff // dp, d)
    down_t = dot_tn(df, gg).astype(BF16).reshape(dp, d // dp * (ff // d), d)
    query_t = dot_tn(dq, nx).astype(BF16).reshape(dp, inner // dp, d)
    kv_t = dot_tn(dkv, kin).astype(BF16).reshape(2, dp, inner // dp, d)
    output_t = dot_tn(da, att).astype(BF16).reshape(dp, d // dp * inner // d, d)
    norm_t = norm_grads.astype(BF16).reshape(8, dp, d // dp).swapaxes(0, 1)
    norm_t = jnp.pad(norm_t.reshape(dp, 1, 8 * d // dp), ((0, 0), (0, 15), (0, d - 8 * d // dp)))
    packed = jnp.concatenate([up_t, down_t, query_t, kv_t[0], kv_t[1], output_t, norm_t], axis=1)
    summed = lax.psum_scatter(packed, "dp", scatter_dimension=0, tiled=False).astype(F32)
    sizes = [ff // dp, ff // dp, inner // dp, inner // dp, inner // dp, inner // dp]
    parts, at = [], 0
    for size in sizes:
        parts.append(summed[at : at + size])
        at += size
    norm_part = summed[at, : 8 * d // dp].reshape(8, d // dp)
    down_g = parts[1].reshape(d // dp, ff).T
    out_g = parts[5].reshape(d // dp, inner).T
    attn = [part.T for part in parts[2:5]]
    return came, med_came, attn, down_g, out_g, parts[0].T, norm_part


def local(
    latents,
    media_tokens,
    image_counts,
    cotangent,
    query_weight,
    key_weight,
    value_weight,
    output_weight,
    up_weight,
    down_weight,
    media_gain,
    media_bias,
    latent_gain,
    latent_bias,
    feed_gain,
    feed_bias,
):
    micro_count, samples, slot_count, lat, half = latents.shape
    patches = media_tokens.shape[3]
    images = micro_count * samples * slot_count
    d = 2 * half
    dp = lax.axis_size("dp")
    section = lax.axis_index("section")
    weights = (
        query_weight[0],
        key_weight[0],
        value_weight[0],
        output_weight[0],
        up_weight[0],
        down_weight[0],
    )
    norms = (media_gain, media_bias, latent_gain, latent_bias, feed_gain, feed_bias)
    inner, ff = query_weight.shape[2], up_weight.shape[2]
    gg, dh, nf, df, att, da, dq, kin, dkv, res, latgrad, dmed, norm_grads = run_layers(
        latents.reshape(images, lat, half),
        media_tokens.reshape(images, patches, half),
        cotangent.reshape(images, lat, half),
        image_counts.reshape(-1),
        weights,
        norms,
        slot_count,
    )
    lead = (micro_count, samples, slot_count)
    saved = (gg, dh, nf, df, att, da, dq, kin, dkv)
    fits = dp % 4 == 0 and ff // dp % 256 == 0 and half % (ff // dp // 2) == 0
    fits = fits and inner // dp % 16 == 0 and d // dp * inner % d == 0 and ff // d % 2 == 0
    if fits:
        main, attn_t, came, med_came = run_reduce(saved, norm_grads, res, latgrad, dmed, dp)
        outs = run_outputs(dmed, med_came, res, latgrad, came, main, attn_t, section, dp)
        resampled, latent_grad, media_grad, up_g, down_t, *parts = outs
        return (
            resampled.reshape(lead + (lat, half)),
            latent_grad.reshape(lead + (lat, half)),
            media_grad.reshape(lead + (patches, half)),
            parts[0].T[None],
            parts[1].T[None],
            parts[2].T[None],
            parts[3].T[None],
            up_g[None],
            down_t.T[None],
            *parts[4:],
        )
    came, med_came, parts, down_g, out_g, up_g, norm_part = plain_reduce(
        saved, norm_grads, res, latgrad, dmed, dp
    )
    resampled = jnp.where(section == 0, came, res[..., half:])
    latent_grad = jnp.where(section == 0, latgrad[..., :half], came).astype(F32)
    med_mine = lax.dynamic_index_in_dim(dmed, section, 0, keepdims=False)
    media_grad = med_mine.astype(F32) + med_came.astype(F32)
    return (
        resampled.reshape(lead + (lat, half)),
        latent_grad.reshape(lead + (lat, half)),
        media_grad.reshape(lead + (patches, half)),
        parts[0][None],
        parts[1][None],
        parts[2][None],
        out_g[None],
        up_g[None],
        down_g[None],
        *[norm_part[i][None] for i in range(6)],
    )


def solution(mesh):
    feature = P(None, "dp", None, None, "section")
    weight = P("section", None, None)
    vector = P("section", None)
    in_specs = (feature, feature, P(None, "dp"), feature) + (weight,) * 6 + (vector,) * 6
    out_specs = (feature,) * 3 + (P("section", None, "dp"),) * 6 + (P("section", "dp"),) * 6
    return jax.shard_map(
        local, mesh=mesh, in_specs=in_specs, out_specs=out_specs, check_vma=False
    )
```

```python
import functools

import jax
import jax.numpy as jnp
from jax import lax
from jax.experimental import pallas as pl
from jax.experimental.pallas import tpu as pltpu
from jax.sharding import PartitionSpec as P

DH = 64
EPS = 1e-05
QUERY_SCALE = 0.125
QUAD = 4
GROUP = 2
F32, BF16 = jnp.float32, jnp.bfloat16


def dot(a, b):
    return lax.dot_general(a, b, (((1,), (0,)), ((), ())), preferred_element_type=F32)


def dot_nt(a, b):
    return lax.dot_general(a, b, (((1,), (1,)), ((), ())), preferred_element_type=F32)


def dot_tn(a, b):
    return lax.dot_general(a, b, (((0,), (0,)), ((), ())), preferred_element_type=F32)


def standardize(rows):
    centered = rows - jnp.mean(rows, -1, keepdims=True)
    inverse = lax.rsqrt(jnp.mean(centered * centered, -1, keepdims=True) + EPS)
    return centered * inverse, inverse


def gelu_parts(hidden):
    t = 1.0 / (1.0 + (0.3275911 * 0.5**0.5) * jnp.abs(hidden))
    bell = jnp.exp(hidden * hidden * -0.5)
    series = 0.5 * 1.061405429
    for term in (-1.453152027, 1.421413741, -0.284496736, 0.254829592):
        series = series * t + 0.5 * term
    tail = series * t * bell
    below = jnp.where(hidden < 0.0, tail, 1.0 - tail)
    return hidden * below, below + hidden * bell * 0.3989422804014327


def norm_back(grads, standard, inverse, gain):
    scaled = grads * gain
    return inverse * (
        scaled
        - jnp.mean(scaled, -1, keepdims=True)
        - standard * jnp.mean(scaled * standard, -1, keepdims=True)
    )


def layers_kernel(
    dims,
    counts,
    media_gain,
    media_bias,
    latent_gain,
    latent_bias,
    feed_gain,
    feed_bias,
    latents,
    media,
    cotangent,
    wq_hbm,
    wk_hbm,
    wv_hbm,
    wo_hbm,
    up_hbm,
    down_hbm,
    gg_out,
    dh_out,
    nf_out,
    df_out,
    att_out,
    da_out,
    dq_out,
    kin_out,
    dkv_out,
    rows_out,
    latgrad_out,
    dmed_out,
    norm_grads,
    wq,
    wkv,
    wo,
    up,
    down,
    med_in,
    x_in,
    g_in,
    q_keep,
    kv_keep,
    pr_keep,
    x1_keep,
    slope_keep,
    y_stage,
    dy_stage,
    kin_st,
    dkv_st,
    gg_st,
    dh_st,
    nf_st,
    df_st,
    att_st,
    da_st,
    dq_st,
    dmed_st,
    acc,
    dkin,
    w_sem,
    own_sem,
    xown_sem,
    gown_sem,
    med_send,
    med_recv,
    x_send,
    x_recv,
    g_send,
    g_recv,
    f_sem,
    b_sem,
    row_sem,
    lg_sem,
):
    chunks, patches, lat, d, inner, ff, slots = dims
    keys = patches + lat
    rows = GROUP * lat
    half = d // 2
    quads = inner // (QUAD * DH)
    qw = QUAD * DH
    sec = lax.axis_index("section")
    peer = 1 - sec
    first = sec == 0
    mine = pl.ds(pl.multiple_of(sec * half, half), half)
    theirs = pl.ds(pl.multiple_of(peer * half, half), half)
    there = {"section": peer}

    def remote(src, dst, send, recv):
        return pltpu.make_async_remote_copy(
            src_ref=src,
            dst_ref=dst,
            send_sem=send,
            recv_sem=recv,
            device_id=there,
            device_id_type=pl.DeviceIdType.MESH,
        )

    def group(c):
        return pl.ds(c * GROUP, GROUP)

    images = chunks * GROUP

    def med_copy(n):
        return remote(
            media.at[n], med_in.at[n, :, mine], med_send.at[n], med_recv.at[n]
        )

    def med_arrival(n):
        return remote(
            media.at[n], med_in.at[n, :, theirs], med_send.at[n], med_recv.at[n]
        )

    def half_copy(src, dst, send, recv, c, where):
        return remote(src.at[group(c)], dst.at[group(c), :, where], send.at[c], recv.at[c])

    def whole_copy(src, dst, send, recv, c):
        return remote(src.at[group(c)], dst.at[group(c)], send.at[c], recv.at[c])

    def med_own(c):
        return pltpu.make_async_copy(
            media.at[group(c)], med_in.at[group(c), :, mine], own_sem.at[c]
        )

    lat_own = pltpu.make_async_copy(latents, x_in.at[:, :, mine], xown_sem)
    cot_own = pltpu.make_async_copy(cotangent, g_in.at[:, :, mine], gown_sem)

    weight_copies = [
        pltpu.make_async_copy(wk_hbm, wkv.at[:, pl.ds(0, inner)], w_sem.at[0]),
        pltpu.make_async_copy(wv_hbm, wkv.at[:, pl.ds(inner, inner)], w_sem.at[1]),
        pltpu.make_async_copy(wq_hbm, wq, w_sem.at[2]),
        pltpu.make_async_copy(wo_hbm, wo, w_sem.at[3]),
        pltpu.make_async_copy(up_hbm, up, w_sem.at[4]),
        pltpu.make_async_copy(down_hbm, down, w_sem.at[5]),
    ]

    barrier = pltpu.get_barrier_semaphore()
    pl.semaphore_signal(
        barrier, inc=1, device_id=there, device_id_type=pl.DeviceIdType.MESH
    )
    pl.semaphore_wait(barrier, 1)

    for c in range(chunks):
        med_own(c).start()

    @pl.when(first)
    def _():
        lat_own.start()
        for n in range(GROUP):
            med_copy(n).start()
        half_copy(cotangent, g_in, g_send, g_recv, 0, mine).start()

    @pl.when(jnp.logical_not(first))
    def _():
        cot_own.start()
        half_copy(latents, x_in, x_send, x_recv, 0, mine).start()
        for n in range(GROUP):
            med_copy(n).start()

    for copy in weight_copies:
        copy.start()
    norm_grads[...] = jnp.zeros_like(norm_grads)

    early = min(2 * GROUP, images)

    @pl.when(first)
    def _():
        lat_own.wait()
        for n in range(GROUP, early):
            med_copy(n - GROUP).wait_send()
            med_copy(n).start()

    @pl.when(jnp.logical_not(first))
    def _():
        cot_own.wait()
        for n in range(GROUP, early):
            med_copy(n - GROUP).wait_send()
            if n % GROUP == 0:
                half_copy(latents, x_in, x_send, x_recv, n // GROUP, mine).start()
            med_copy(n).start()

    def lane_head(n, h):
        return (lax.broadcasted_iota(jnp.int32, (n, qw), 1) // DH) == h

    def spread(quad_rows):
        return jnp.concatenate(
            [
                jnp.where(lane_head(lat, h), quad_rows, jnp.zeros_like(quad_rows))
                for h in range(QUAD)
            ],
            axis=0,
        )

    def gather_heads(stacked):
        total = jnp.where(lane_head(lat, 0), stacked[:lat], 0.0)
        for h in range(1, QUAD):
            total = total + jnp.where(
                lane_head(lat, h), stacked[h * lat : (h + 1) * lat], 0.0
            )
        return total

    def f_copies(c):
        r = pl.ds(c * rows, rows)
        return [
            pltpu.make_async_copy(gg_st, gg_out.at[:, r], f_sem.at[0]),
            pltpu.make_async_copy(nf_st, nf_out.at[r], f_sem.at[1]),
            pltpu.make_async_copy(att_st, att_out.at[r], f_sem.at[2]),
            pltpu.make_async_copy(
                kin_st, kin_out.at[pl.ds(c * GROUP * keys, GROUP * keys)], f_sem.at[3]
            ),
        ]

    def b_copies(c):
        r = pl.ds(c * rows, rows)
        return [
            pltpu.make_async_copy(dh_st, dh_out.at[:, r], b_sem.at[0]),
            pltpu.make_async_copy(df_st, df_out.at[r], b_sem.at[1]),
            pltpu.make_async_copy(da_st, da_out.at[r], b_sem.at[2]),
            pltpu.make_async_copy(dq_st, dq_out.at[r], b_sem.at[3]),
            pltpu.make_async_copy(
                dkv_st, dkv_out.at[pl.ds(c * GROUP * keys, GROUP * keys)], b_sem.at[4]
            ),
            pltpu.make_async_copy(dmed_st.at[0], dmed_out.at[0, group(c)], b_sem.at[5]),
            pltpu.make_async_copy(dmed_st.at[1], dmed_out.at[1, group(c)], b_sem.at[6]),
        ]

    def row_copy(c):
        return pltpu.make_async_copy(
            y_stage.at[group(c)], rows_out.at[group(c)], row_sem.at[c]
        )

    def lg_copy(c):
        return pltpu.make_async_copy(
            dy_stage.at[group(c)], latgrad_out.at[group(c)], lg_sem.at[c]
        )

    def mask_of(image):
        sample = image // slots
        return jnp.where(image - sample * slots < counts[sample], 1.0, 0.0)

    step_rows = 64
    ff_tile = d // 2

    def forward(c):
        @pl.when(c > 0)
        def _():
            for copy in f_copies(c - 1):
                copy.wait()

        med_own(c).wait()
        for i in range(GROUP):
            med_arrival(c * GROUP + i).wait_recv()

        for i in range(GROUP):

            def media_rows(k, carry, i=i):
                r = pl.ds(pl.multiple_of(k * step_rows, step_rows), step_rows)
                standard, _ = standardize(med_in[c * GROUP + i, r, :].astype(F32))
                to = pl.ds(pl.multiple_of(i * keys + k * step_rows, step_rows), step_rows)
                kin_st[to, :] = (standard * media_gain[...] + media_bias[...]).astype(BF16)
                return carry

            lax.fori_loop(0, patches // step_rows, media_rows, 0, unroll=True)

        @pl.when(first)
        def _():
            half_copy(latents, x_in, x_send, x_recv, c, theirs).wait_recv()

        @pl.when(jnp.logical_not(first))
        def _():
            whole_copy(y_stage, x_in, x_send, x_recv, c).wait_recv()

        for i in range(GROUP):
            standard, _ = standardize(x_in[c * GROUP + i].astype(F32))
            kin_st[i * keys + patches : (i + 1) * keys, :] = (
                standard * latent_gain[...] + latent_bias[...]
            ).astype(BF16)

        @pl.when(c == 0)
        def _():
            for copy in weight_copies[:4]:
                copy.wait()

        n_tile = 256

        def kv_tile(j, carry):
            cols = pl.ds(pl.multiple_of(j * n_tile, n_tile), n_tile)
            kv_keep[c, :, cols] = dot(kin_st[...], wkv[:, cols]).astype(BF16)
            return carry

        lax.fori_loop(0, 2 * inner // n_tile, kv_tile, 0)
        nx = jnp.concatenate(
            [kin_st[i * keys + patches : (i + 1) * keys, :] for i in range(GROUP)], axis=0
        )
        q_keep[c] = (dot(nx, wq[...]) * QUERY_SCALE).astype(BF16)

        for i in range(GROUP):
            for g in range(quads):
                lanes = slice(g * qw, (g + 1) * qw)
                r = slice(i * keys, (i + 1) * keys)
                stack = spread(q_keep[c, i * lat : (i + 1) * lat, lanes])
                scores = dot_nt(stack, kv_keep[c, r, lanes])
                top = jnp.max(scores, -1, keepdims=True)
                powers = jnp.exp(scores - top)
                probs = (powers * (1.0 / jnp.sum(powers, -1, keepdims=True))).astype(BF16)
                pr_keep[c, i * quads + g] = probs
                mixed = dot(probs, kv_keep[c, r, inner + g * qw : inner + (g + 1) * qw])
                att_st[i * lat : (i + 1) * lat, lanes] = gather_heads(mixed).astype(BF16)

        x1 = x_in[group(c)].reshape(rows, d).astype(F32) + dot(att_st[...], wo[...])
        x1_keep[c] = x1
        standard, _ = standardize(x1)
        nf_st[...] = (standard * feed_gain[...] + feed_bias[...]).astype(BF16)

        @pl.when(c == 0)
        def _():
            for copy in weight_copies[4:]:
                copy.wait()

        acc[...] = x1

        tiles = ff // ff_tile
        normed = nf_st[...]
        hidden = dot(normed, up[:, :ff_tile])
        for j in range(tiles):
            if j + 1 < tiles:
                ahead = dot(normed, up[:, (j + 1) * ff_tile : (j + 2) * ff_tile])
            active, slope = gelu_parts(hidden)
            slope_keep[c, :, j * ff_tile : (j + 1) * ff_tile] = slope.astype(BF16)
            active = active.astype(BF16)
            gg_st[j] = active
            acc[...] += dot(active, down[j * ff_tile : (j + 1) * ff_tile, :])
            hidden = ahead

        for i in range(GROUP):
            scale = jnp.where(first, 1.0, mask_of(c * GROUP + i))
            y_stage[c * GROUP + i] = (acc[i * lat : (i + 1) * lat, :] * scale).astype(BF16)

        @pl.when(first)
        def _():
            whole_copy(y_stage, x_in, x_send, x_recv, c).start()

            @pl.when(c + 2 < chunks)
            def _():
                for i in range(GROUP):
                    med_copy((c + 2) * GROUP + i).start()

            @pl.when(c + 1 < chunks)
            def _():
                half_copy(cotangent, g_in, g_send, g_recv, c + 1, mine).start()

        @pl.when(jnp.logical_not(first))
        def _():
            row_copy(c).start()

        for copy in f_copies(c):
            copy.start()

    def backward(c):
        @pl.when(c > 0)
        def _():
            for copy in b_copies(c - 1):
                copy.wait()

        @pl.when(first)
        def _():
            whole_copy(dy_stage, g_in, g_send, g_recv, c).wait_recv()

        @pl.when(jnp.logical_not(first))
        def _():
            half_copy(cotangent, g_in, g_send, g_recv, c, theirs).wait_recv()

        for i in range(GROUP):
            scale = jnp.where(first, 1.0, mask_of(c * GROUP + i))
            df_st[i * lat : (i + 1) * lat, :] = (
                g_in[c * GROUP + i].astype(F32) * scale
            ).astype(BF16)
        tiles = ff // ff_tile
        grads_low = df_st[...]
        dg = dot_nt(grads_low, down[:ff_tile, :])
        for j in range(tiles):
            if j + 1 < tiles:
                ahead = dot_nt(grads_low, down[(j + 1) * ff_tile : (j + 2) * ff_tile, :])
            slope = slope_keep[c, :, j * ff_tile : (j + 1) * ff_tile].astype(F32)
            dh = (dg * slope).astype(BF16)
            dh_st[j] = dh
            more = dot_nt(dh, up[:, j * ff_tile : (j + 1) * ff_tile])
            acc[...] = more if j == 0 else acc[...] + more
            dg = ahead
        standard, inverse = standardize(x1_keep[c])
        dnf = acc[...]
        norm_grads[4:5, :] += jnp.sum(dnf * standard, axis=0, keepdims=True)
        norm_grads[5:6, :] += jnp.sum(dnf, axis=0, keepdims=True)
        dx1 = df_st[...].astype(F32) + norm_back(dnf, standard, inverse, feed_gain[...])
        acc[...] = dx1
        da_st[...] = dx1.astype(BF16)
        datt = dot_nt(da_st[...], wo[...]).astype(BF16)
        for i in range(GROUP):
            for g in range(quads):
                lanes = slice(g * qw, (g + 1) * qw)
                vlanes = slice(inner + g * qw, inner + (g + 1) * qw)
                r = slice(i * keys, (i + 1) * keys)
                lr = slice(i * lat, (i + 1) * lat)
                stack = spread(datt[lr, lanes])
                dp = dot_nt(stack, kv_keep[c, r, vlanes])
                probs = pr_keep[c, i * quads + g]
                dkv_st[r, vlanes] = dot_tn(probs, stack).astype(BF16)
                wide = probs.astype(F32)
                ds = (wide * (dp - jnp.sum(wide * dp, -1, keepdims=True))).astype(BF16)
                dkv_st[r, lanes] = dot_tn(ds, spread(q_keep[c, lr, lanes])).astype(BF16)
                mixed = gather_heads(dot(ds, kv_keep[c, r, lanes])).astype(BF16)
                dq_st[lr, lanes] = (mixed.astype(F32) * QUERY_SCALE).astype(BF16)

        d_lat = jnp.concatenate(
            [dkv_st[i * keys + patches : (i + 1) * keys, :] for i in range(GROUP)], axis=0
        )
        dnx = dot_nt(d_lat, wkv[...]) + dot_nt(dq_st[...], wq[...])
        standard, inverse = standardize(x_in[group(c)].reshape(rows, d).astype(F32))
        norm_grads[2:3, :] += jnp.sum(dnx * standard, axis=0, keepdims=True)
        norm_grads[3:4, :] += jnp.sum(dnx, axis=0, keepdims=True)
        dx = acc[...] + norm_back(dnx, standard, inverse, latent_gain[...])
        dy_stage[group(c)] = dx.astype(BF16).reshape(GROUP, lat, d)

        @pl.when(first)
        def _():
            lg_copy(c).start()

        @pl.when(jnp.logical_not(first))
        def _():
            whole_copy(dy_stage, g_in, g_send, g_recv, c).start()

        for i in range(GROUP):
            dkin[...] = dot_nt(dkv_st[i * keys : i * keys + patches, :], wkv[...])

            def media_rows(k, carry, i=i):
                r = pl.ds(pl.multiple_of(k * step_rows, step_rows), step_rows)
                standard, inverse = standardize(med_in[c * GROUP + i, r, :].astype(F32))
                grads = dkin[r, :]
                norm_grads[0:1, :] += jnp.sum(grads * standard, axis=0, keepdims=True)
                norm_grads[1:2, :] += jnp.sum(grads, axis=0, keepdims=True)
                out = norm_back(grads, standard, inverse, media_gain[...]).astype(BF16)
                dmed_st[0, i, r, :] = out[:, :half]
                dmed_st[1, i, r, :] = out[:, half:]
                return carry

            lax.fori_loop(0, patches // step_rows, media_rows, 0, unroll=True)

        for copy in b_copies(c):
            copy.start()

    def step(t, carry):
        second = t // 2
        is_forward = jnp.where(first, t < chunks, t - second * 2 == 0)

        @pl.when(jnp.logical_not(first) & (t + 2 < chunks))
        def _():
            half_copy(latents, x_in, x_send, x_recv, t + 2, mine).start()
            for i in range(GROUP):
                med_copy((t + 2) * GROUP + i).start()

        c = jnp.where(first, jnp.where(t < chunks, t, t - chunks), second)

        @pl.when(is_forward)
        def _():
            forward(c)

        @pl.when(jnp.logical_not(is_forward))
        def _():
            backward(c)

        return carry

    lax.fori_loop(0, 2 * chunks, step, 0)

    for copy in f_copies(chunks - 1) + b_copies(chunks - 1):
        copy.wait()

    @pl.when(first)
    def _():
        for n in range(early - GROUP, images):
            med_copy(n).wait_send()
        for c in range(chunks):
            lg_copy(c).wait()
            whole_copy(y_stage, x_in, x_send, x_recv, c).wait_send()
            half_copy(cotangent, g_in, g_send, g_recv, c, mine).wait_send()

    @pl.when(jnp.logical_not(first))
    def _():
        for n in range(early - GROUP, images):
            med_copy(n).wait_send()
        for c in range(chunks):
            row_copy(c).wait()
            half_copy(latents, x_in, x_send, x_recv, c, mine).wait_send()
            whole_copy(dy_stage, g_in, g_send, g_recv, c).wait_send()


def run_layers(latents, media, cotangent, counts, weights, norms, slots):
    images, lat, half = latents.shape
    patches = media.shape[1]
    d = 2 * half
    wq, wk, wv, wo, up, down = weights
    inner, ff = wq.shape[1], up.shape[1]
    chunks = images // GROUP
    keys = patches + lat
    rows = GROUP * lat
    quads = inner // (QUAD * DH)
    dims = (chunks, patches, lat, d, inner, ff, slots)
    total, wide = images * lat, images * keys

    def out(*shape, dtype=BF16):
        return jax.ShapeDtypeStruct(shape, dtype)

    any_spec = pl.BlockSpec(memory_space=pl.ANY)
    vmem_spec = pl.BlockSpec(memory_space=pltpu.VMEM)
    dma = pltpu.SemaphoreType.DMA
    return pl.pallas_call(
        functools.partial(layers_kernel, dims),
        out_shape=(
            out(2 * ff // d, total, half),
            out(2 * ff // d, total, half),
            out(total, d),
            out(total, d),
            out(total, inner),
            out(total, d),
            out(total, inner),
            out(wide, d),
            out(wide, 2 * inner),
            out(images, lat, d),
            out(images, lat, d),
            out(2, images, patches, half),
            out(8, d, dtype=F32),
        ),
        in_specs=[pl.BlockSpec(memory_space=pltpu.SMEM)] + [vmem_spec] * 6 + [any_spec] * 9,
        out_specs=(any_spec,) * 12 + (vmem_spec,),
        scratch_shapes=[
            pltpu.VMEM((d, inner), BF16),
            pltpu.VMEM((d, 2 * inner), BF16),
            pltpu.VMEM((inner, d), BF16),
            pltpu.VMEM((d, ff), BF16),
            pltpu.VMEM((ff, d), BF16),
            pltpu.VMEM((images, patches, d), BF16),
            pltpu.VMEM((images, lat, d), BF16),
            pltpu.VMEM((images, lat, d), BF16),
            pltpu.VMEM((chunks, rows, inner), BF16),
            pltpu.VMEM((chunks, GROUP * keys, 2 * inner), BF16),
            pltpu.VMEM((chunks, GROUP * quads, QUAD * lat, keys), BF16),
            pltpu.VMEM((chunks, rows, d), F32),
            pltpu.VMEM((chunks, rows, ff), BF16),
            pltpu.VMEM((images, lat, d), BF16),
            pltpu.VMEM((images, lat, d), BF16),
            pltpu.VMEM((GROUP * keys, d), BF16),
            pltpu.VMEM((GROUP * keys, 2 * inner), BF16),
            pltpu.VMEM((2 * ff // d, rows, half), BF16),
            pltpu.VMEM((2 * ff // d, rows, half), BF16),
            pltpu.VMEM((rows, d), BF16),
            pltpu.VMEM((rows, d), BF16),
            pltpu.VMEM((rows, inner), BF16),
            pltpu.VMEM((rows, d), BF16),
            pltpu.VMEM((rows, inner), BF16),
            pltpu.VMEM((2, GROUP, patches, half), BF16),
            pltpu.VMEM((rows, d), F32),
            pltpu.VMEM((patches, d), F32),
            dma((6,)),
            dma((chunks,)),
            dma,
            dma,
            dma((images,)),
            dma((images,)),
            dma((chunks,)),
            dma((chunks,)),
            dma((chunks,)),
            dma((chunks,)),
            dma((4,)),
            dma((7,)),
            dma((chunks,)),
            dma((chunks,)),
        ],
        compiler_params=pltpu.CompilerParams(
            collective_id=0, has_side_effects=True, vmem_limit_bytes=63 * 2**20
        ),
        cost_estimate=pl.CostEstimate(
            flops=4 * images * 960_000_000, bytes_accessed=80_000_000, transcendentals=0
        ),
        name="layers",
    )(counts, *norms, latents, media, cotangent, wq, wk, wv, wo, up, down)


def reduce_kernel(
    dims,
    norm_grads,
    gg,
    dh,
    nf,
    df,
    att,
    da,
    dq,
    kin,
    dkv,
    rows_in,
    latgrad,
    dmed,
    main_out,
    attn_out,
    came,
    med_came,
    g_up1,
    g_up0,
    g_down0,
    g_low,
    g_high,
    g_attn,
    core_slots,
    x_up1,
    x_up0,
    x_down0,
    x_low,
    x_high,
    x_attn,
    z_up1,
    z_up0,
    z_down0,
    z_low,
    z_high,
    z_attn,
    buf_a,
    buf_b,
    flipped,
    att_v,
    dq_v,
    big_a,
    dh_v,
    big_b,
    stage,
    attn_stage,
    load_sem,
    core_send,
    core_recv,
    x_send,
    x_recv,
    zr_send,
    zr_recv,
    zl_send,
    zl_recv,
    y_send,
    y_recv,
    credit,
    main_sem,
    attn_sem,
):
    images, lat, patches, d, inner, ff, dp = dims
    line = dp // 4
    keys = lat + patches
    total = images * lat
    block = ff // dp // 2
    half = d // 2
    blocks = ff // half
    me = lax.axis_index("dp")
    sec = lax.axis_index("section")
    z = me // 4
    x = me // 2 - z * 2
    c = me - (me // 2) * 2
    sibling = {"dp": me + 1 - 2 * c}
    across = {"dp": me + 2 - 4 * x}
    ahead = {"dp": jnp.minimum(me + 4, dp - 4 + (me - z * 4))}
    behind = {"dp": jnp.maximum(me - 4, me - z * 4)}
    peer = {"section": 1 - sec}
    has_left, has_right = z > 0, z < line - 1
    mesh_ids = pl.DeviceIdType.MESH

    def place(dest):
        return dest % 2, (dest // 2) % 2, dest // 4

    def remote(src, dst, send, recv, device):
        return pltpu.make_async_remote_copy(
            src_ref=src,
            dst_ref=dst,
            send_sem=send,
            recv_sem=recv,
            device_id=device,
            device_id_type=mesh_ids,
        )

    barrier = pltpu.get_barrier_semaphore()
    for device in (sibling, across, peer):
        pl.semaphore_signal(barrier, inc=1, device_id=device, device_id_type=mesh_ids)

    @pl.when(has_left)
    def _():
        pl.semaphore_signal(barrier, inc=1, device_id=behind, device_id_type=mesh_ids)

    @pl.when(has_right)
    def _():
        pl.semaphore_signal(barrier, inc=1, device_id=ahead, device_id_type=mesh_ids)

    def load(src, dst, k):
        return pltpu.make_async_copy(src, dst, load_sem.at[k])

    part = pl.ds(0, images * keys)
    loads = {
        "nf": load(nf, buf_a, 0),
        "dh": load(dh, dh_v, 1),
        "df": load(df, buf_b, 2),
        "gg": load(gg, big_b, 3),
        "att": load(att, att_v, 4),
        "dq": load(dq, dq_v, 5),
        "da": load(da, buf_a, 6),
        "kin": load(kin, big_a, 7),
        "dk": load(dkv.at[:, pl.ds(0, inner)], big_b.at[part], 8),
        "dv": load(dkv.at[:, pl.ds(inner, inner)], big_b.at[part], 9 + images),
    }
    nx_loads = [
        load(kin.at[pl.ds(i * keys + patches, lat)], buf_b.at[pl.ds(i * lat, lat)], 9 + i)
        for i in range(images)
    ]
    for name in ("nf", "dh"):
        loads[name].start()

    pl.semaphore_wait(
        barrier, 3 + jnp.where(has_left, 1, 0) + jnp.where(has_right, 1, 0)
    )

    def out_rows(src, lanes):
        return remote(src.at[:, :, lanes], came, y_send.at[0], y_recv.at[0], peer)

    out_first = out_rows(latgrad, pl.ds(half, half))
    out_second = out_rows(rows_in, pl.ds(0, half))
    out_media = remote(dmed.at[1 - sec], med_came, y_send.at[1], y_recv.at[1], peer)

    @pl.when(sec == 0)
    def _():
        out_first.start()

    @pl.when(sec == 1)
    def _():
        out_second.start()

    out_media.start()

    grads = [g_up1, g_up0, g_down0, g_low, g_high, g_attn]
    count = len(grads)
    core_in = [
        core_slots.at[n % 2, :, :, pl.ds(0, grads[n].shape[3])] for n in range(count)
    ]
    x_in = [x_up1, x_up0, x_down0, x_low, x_high, x_attn]
    z_in = [z_up1, z_up0, z_down0, z_low, z_high, z_attn]
    z_first = 0

    def up_piece(h):
        wide = ff // dp
        groups = half // block
        for j in range(blocks):
            tile = dot(
                flipped[h * half : (h + 1) * half, :], dh_v[j * total : (j + 1) * total, :]
            ).astype(BF16)
            for i in range(half // wide):
                pc, px, pz = place(j * (half // wide) + i)
                for k in range(groups):
                    grads[1 - h][pc, px, pz, :, k * wide : (k + 1) * wide] = tile[
                        k * block : (k + 1) * block, i * wide : (i + 1) * wide
                    ]

    def down_piece(p):
        own = d // dp
        tiles = range(blocks // 2) if p == 2 else range(blocks // 4)
        start = 0 if p == 2 else (p - 1) * (blocks // 4)
        for k in tiles:
            j = start + k
            at = k * half
            r = slice(at // d * own, at // d * own + own)
            lanes = slice(at % d, at % d + half)
            for m in range(2):
                tile = dot(
                    flipped[m * half : (m + 1) * half, :], big_b[j * total : (j + 1) * total, :]
                ).astype(BF16)
                for i in range(half // own):
                    pc, px, pz = place(m * (half // own) + i)
                    grads[p][pc, px, pz, r, lanes] = tile[i * own : (i + 1) * own, :]

    def attn_piece():
        own = inner // dp
        lo = inner // 2

        def store(n, make):
            for m in range(2):
                tile = make(slice(m * lo, (m + 1) * lo)).astype(BF16)
                for i in range(lo // own):
                    pc, px, pz = place(m * (lo // own) + i)
                    g_attn[pc, px, pz, n * own : (n + 1) * own, :] = tile[
                        i * own : (i + 1) * own, :
                    ]

        for copy in nx_loads:
            copy.wait()
        store(0, lambda m: dot_tn(dq_v[:, m], buf_b[...]))
        loads["kin"].wait()
        loads["dk"].wait()
        store(1, lambda m: dot_tn(big_b[: images * keys, m], big_a[...]))
        loads["dv"].start()
        loads["dv"].wait()
        store(2, lambda m: dot_tn(big_b[: images * keys, m], big_a[...]))
        loads["da"].wait()
        out_own = d // dp
        for m in range(2):
            tile = dot_tn(buf_a[:, m * half : (m + 1) * half], att_v[...]).astype(BF16)
            for i in range(half // out_own):
                pc, px, pz = place(m * (half // out_own) + i)
                rest = tile[i * out_own : (i + 1) * out_own, :]
                g_attn[pc, px, pz, 3 * own : 4 * own, :inner] = rest[:own]
                g_attn[pc, px, pz, 3 * own : 4 * own, inner:] = rest[own:]
        lanes = 128
        for dest in range(dp):
            pc, px, pz = place(dest)
            at = (dest * (d // dp)) // lanes * lanes
            sums = norm_grads[:, at : at + lanes]
            g_attn[pc, px, pz, 4 * own :, :] = jnp.zeros((16, d), BF16)
            g_attn[pc, px, pz, 4 * own :, :lanes] = jnp.concatenate(
                [sums, jnp.zeros_like(sums)], axis=0
            ).astype(BF16)

    def core_copy(p):
        return remote(grads[p].at[1 - c], core_in[p], core_send.at[p], core_recv.at[p], sibling)

    def x_copy(p):
        if p == z_first:
            src = grads[p].at[c, 1 - x, z]
        else:
            src = grads[p].at[c, 1 - x]
        return remote(src, x_in[p], x_send.at[p], x_recv.at[p], across)

    def spot(p, t):
        if p == z_first:
            return grads[p].at[c, :, t]
        return grads[p].at[c, x, t]

    def right_copy(p, t):
        k = p * line + t
        return remote(spot(p, t), z_in[p].at[t + 1], zr_send.at[k], zr_recv.at[k], ahead)

    def left_copy(p, t):
        k = p * line + t
        return remote(spot(p, t), z_in[p].at[t], zl_send.at[k], zl_recv.at[k], behind)

    def add_into(target, source):
        target[...] = (target[...].astype(F32) + source[...].astype(F32)).astype(BF16)

    def core_add(p):
        core_copy(p).wait_recv()

        def body(n, carry):
            xx = n // line
            zz = n - xx * line
            add_into(grads[p].at[c, xx, zz], core_in[p].at[xx, zz])
            return carry

        lax.fori_loop(0, 2 * line, body, 0)

    def x_add(p):
        x_copy(p).wait_recv()

        def body(zz, carry):
            add_into(grads[p].at[c, x, zz], x_in[p].at[zz])
            return carry

        lax.fori_loop(0, line, body, 0)

    def z_ends(p):
        @pl.when(z == 0)
        def _():
            for t in range(line - 1, 0, -1):
                right_copy(p, t).start()

        @pl.when(z == line - 1)
        def _():
            for t in range(line - 1):
                left_copy(p, t).start()

    def z_phase(p, k):
        t = line - 1 - k

        def forward_right():
            @pl.when(has_left & (z < t))
            def _():
                right_copy(p, t).wait_recv()
                add_into(spot(p, t), z_in[p].at[t + 1])
                right_copy(p, t).start()

        def forward_left():
            @pl.when(has_right & (z > k))
            def _():
                left_copy(p, k).wait_recv()
                add_into(spot(p, k), z_in[p].at[k])
                left_copy(p, k).start()

        @pl.when(z < line // 2)
        def _():
            forward_right()
            forward_left()

        @pl.when(z >= line // 2)
        def _():
            forward_left()
            forward_right()

    def z_own(p):
        @pl.when(has_left)
        def _():
            for t in range(1, line):

                @pl.when(z == t)
                def _():
                    right_copy(p, t).wait_recv()
                    add_into(spot(p, t), z_in[p].at[t + 1])

        @pl.when(has_right)
        def _():
            for t in range(line - 1):

                @pl.when(z == t)
                def _():
                    left_copy(p, t).wait_recv()
                    add_into(spot(p, t), z_in[p].at[t])

    rows_of = [(block, block), (0, block), (2 * block, block), (3 * block, block // 2)]
    rows_of.append((3 * block + block // 2, block // 2))

    def main_copy(p):
        at, tall = rows_of[p]
        return pltpu.make_async_copy(
            stage.at[pl.ds(0, tall)], main_out.at[pl.ds(at, tall)], main_sem.at[p]
        )

    attn_copy = pltpu.make_async_copy(attn_stage, attn_out, attn_sem)
    staged = []

    def finish(p):
        result = grads[p].at[c, x, z][...].astype(F32)
        if p == z_first:
            result = result + x_in[p][...].astype(F32)
        if p == count - 1:
            attn_stage[...] = result
            attn_copy.start()
        else:
            if staged:
                main_copy(staged.pop()).wait()
            stage[: rows_of[p][1], :] = result
            main_copy(p).start()
            staged.append(p)

    def give_credit():
        pl.semaphore_signal(credit, inc=1, device_id=sibling, device_id_type=mesh_ids)

    loads["nf"].wait()
    flipped[...] = buf_a[...].T
    loads["da"].start()
    loads["dh"].wait()
    for name in ("df", "gg", "att", "dq", "kin"):
        loads[name].start()
    up_piece(1)
    core_copy(0).start()
    up_piece(0)
    core_copy(1).start()
    core_add(0)
    give_credit()
    z_ends(0)
    loads["df"].wait()
    flipped[...] = buf_b[...].T
    for copy in nx_loads:
        copy.start()
    loads["gg"].wait()
    core_add(1)
    give_credit()
    x_copy(1).start()
    down_piece(2)
    pl.semaphore_wait(credit, 1)
    core_copy(2).start()
    down_piece(3)
    pl.semaphore_wait(credit, 1)
    core_copy(3).start()
    core_add(2)
    give_credit()
    x_copy(2).start()
    z_phase(0, 0)
    down_piece(4)
    pl.semaphore_wait(credit, 1)
    core_copy(4).start()
    loads["dk"].start()
    core_add(3)
    give_credit()
    for k in range(1, line - 1):
        z_phase(0, k)
    loads["att"].wait()
    loads["dq"].wait()
    attn_piece()
    pl.semaphore_wait(credit, 1)
    core_copy(5).start()
    core_add(4)
    z_own(0)
    x_copy(0).start()
    core_add(5)
    order = [1, 2, 5, 3, 4]
    for n, p in enumerate(order):
        x_add(p)
        if n + 2 < len(order):
            x_copy(order[n + 2]).start()
        z_ends(p)
        if n > 0:
            z_own(order[n - 1])
            finish(order[n - 1])
        for k in range(line - 1):
            z_phase(p, k)
        if n == 1:
            x_copy(0).wait_recv()
            finish(0)
    z_own(order[-1])
    finish(order[-1])
    main_copy(staged.pop()).wait()
    attn_copy.wait()

    for p in range(count):
        core_copy(p).wait_send()
        x_copy(p).wait_send()
        for t in range(1, line):

            @pl.when(z < t)
            def _(p=p, t=t):
                right_copy(p, t).wait_send()

        for t in range(line - 1):

            @pl.when(z > t)
            def _(p=p, t=t):
                left_copy(p, t).wait_send()

    @pl.when(sec == 0)
    def _():
        out_first.wait()

    @pl.when(sec == 1)
    def _():
        out_second.wait()

    out_media.wait()


def run_reduce(saved, norm_grads, res, latgrad, dmed, dp):
    gg, dh, nf, df, att, da, dq, kin, dkv = saved
    images, lat, d = res.shape
    patches, half = dmed.shape[2:]
    inner, ff = att.shape[1], gg.shape[0] * half
    line = dp // 4
    block = ff // dp // 2
    tall = 4 * inner // dp + 16
    dims = (images, lat, patches, d, inner, ff, dp)
    total, wide = images * lat, images * (lat + patches)
    any_spec = pl.BlockSpec(memory_space=pl.ANY)
    vmem_spec = pl.BlockSpec(memory_space=pltpu.VMEM)
    dma = pltpu.SemaphoreType.DMA
    heights = (block, block, block, block // 2, block // 2, tall)
    pieces = len(heights)

    def low(*shape):
        return pltpu.VMEM(shape, BF16)

    return pl.pallas_call(
        functools.partial(reduce_kernel, dims),
        out_shape=(
            jax.ShapeDtypeStruct((4 * block, d), F32),
            jax.ShapeDtypeStruct((tall, d), F32),
            jax.ShapeDtypeStruct((images, lat, half), BF16),
            jax.ShapeDtypeStruct((images, patches, half), BF16),
        ),
        in_specs=[vmem_spec] + [any_spec] * 12,
        out_specs=(any_spec,) * 4,
        scratch_shapes=[
            *[low(2, 2, line, n, d) for n in heights],
            low(2, 2, line, tall, d),
            low(block, d),
            *[low(line, n, d) for n in heights[1:]],
            low(line + 1, 2, block, d),
            *[low(line + 1, n, d) for n in heights[1:]],
            low(total, d),
            low(total, d),
            low(d, total),
            low(total, inner),
            low(total, inner),
            low(wide, d),
            low(2 * ff // d * total, half),
            low(2 * ff // d * total, half),
            pltpu.VMEM((block, d), F32),
            pltpu.VMEM((tall, d), F32),
            dma((10 + images,)),
            dma((pieces,)),
            dma((pieces,)),
            dma((pieces,)),
            dma((pieces,)),
            dma((pieces * line,)),
            dma((pieces * line,)),
            dma((pieces * line,)),
            dma((pieces * line,)),
            dma((2,)),
            dma((2,)),
            pltpu.SemaphoreType.REGULAR,
            dma((pieces - 1,)),
            dma,
        ],
        compiler_params=pltpu.CompilerParams(
            collective_id=1, has_side_effects=True, vmem_limit_bytes=63 * 2**20
        ),
        cost_estimate=pl.CostEstimate(
            flops=2 * images * 960_000_000, bytes_accessed=60_000_000, transcendentals=0
        ),
        name="reduce",
    )(
        norm_grads,
        gg.reshape(-1, half),
        dh.reshape(-1, half),
        nf,
        df,
        att,
        da,
        dq,
        kin,
        dkv,
        res,
        latgrad,
        dmed,
    )


def outputs_kernel(
    dims,
    where,
    media_own,
    media_came,
    rows_in,
    latgrad,
    came,
    main,
    attn,
    resampled,
    latent_grad,
    media_grad,
    up_out,
    down_out,
    query_out,
    key_out,
    value_out,
    output_out,
    *norm_outs,
):
    block, share, own, inner, d, ff, dp = dims
    first = where[0] == 0
    media_grad[...] = media_own[0].astype(F32) + media_came[...].astype(F32)
    resampled[...] = jnp.where(first, came[...], rows_in[...])
    latent_grad[...] = jnp.where(first, latgrad[...], came[...]).astype(F32)

    @pl.when(pl.program_id(0) == 0)
    def _():
        half, wide = d // 2, ff // dp
        for h in range(2):
            for k in range(half // block):
                at = h * half + k * block
                up_out[at : at + block, :] = main[
                    h * block : (h + 1) * block, k * wide : (k + 1) * wide
                ]
        for k in range(ff // d):
            down_out[:, k * d : (k + 1) * d] = main[
                2 * block + k * share : 2 * block + (k + 1) * share, :
            ]
        query_out[...] = attn[:own, :]
        key_out[...] = attn[own : 2 * own, :]
        value_out[...] = attn[2 * own : 3 * own, :]
        output_out[:own, :] = attn[3 * own : 4 * own, :inner]
        output_out[own:, :] = attn[3 * own : 4 * own, inner:]
        sums = attn[4 * own : 4 * own + 8, :128]
        part = sums[:, :share]
        for n in range(1, 128 // share):
            part = jnp.where(where[1] == n, sums[:, n * share : (n + 1) * share], part)
        for n, out in enumerate(norm_outs):
            out[...] = part[n : n + 1, :]


def run_outputs(dmed, med_came, res, latgrad, came, main, attn, section, dp):
    images, lat, d = res.shape
    patches, half = dmed.shape[2:]
    several = 2 if images % 2 == 0 else 1
    block = main.shape[0] // 4
    ff = 2 * block * dp
    share = d // dp
    own = (attn.shape[0] - 16) // 4
    inner = own * dp
    place = jnp.stack([section, lax.axis_index("dp") % (128 // share)]).astype(jnp.int32)

    def whole(*shape):
        return pl.BlockSpec(shape, lambda n, w: (0,) * len(shape))

    def part(rows, lanes=0):
        return pl.BlockSpec((several, rows, half), lambda n, w: (n, 0, lanes))

    small = [(d, ff // dp), (share, ff), (own, d), (own, d), (own, d), (share, inner)]
    small += [(1, share)] * 6
    return pl.pallas_call(
        functools.partial(outputs_kernel, (block, share, own, inner, d, ff, dp)),
        out_shape=[
            jax.ShapeDtypeStruct((images, lat, half), BF16),
            jax.ShapeDtypeStruct((images, lat, half), F32),
            jax.ShapeDtypeStruct((images, patches, half), F32),
        ]
        + [jax.ShapeDtypeStruct(shape, F32) for shape in small],
        grid_spec=pltpu.PrefetchScalarGridSpec(
            num_scalar_prefetch=1,
            grid=(images // several,),
            in_specs=[
                pl.BlockSpec((1, several, patches, half), lambda n, w: (w[0], n, 0, 0)),
                part(patches),
                part(lat, 1),
                part(lat, 0),
                part(lat),
                whole(*main.shape),
                whole(*attn.shape),
            ],
            out_specs=[part(lat), part(lat), part(patches)] + [whole(*shape) for shape in small],
        ),
        compiler_params=pltpu.CompilerParams(vmem_limit_bytes=62 * 2**20),
        name="outputs",
    )(place, dmed, med_came, res, latgrad, came, main, attn)


def plain_reduce(saved, norm_grads, res, latgrad, dmed, dp):
    gg, dh, nf, df, att, da, dq, kin, dkv = saved
    images, lat, d = res.shape
    patches, half = dmed.shape[2:]
    inner, ff = att.shape[1], gg.shape[0] * half
    section = lax.axis_index("section")
    swap = [(0, 1), (1, 0)]
    to_send = jnp.where(section == 0, latgrad[..., half:], res[..., :half])
    came = lax.ppermute(to_send, "section", swap)
    med_theirs = lax.dynamic_index_in_dim(dmed, 1 - section, 0, keepdims=False)
    med_came = lax.ppermute(med_theirs, "section", swap)
    nx = kin.reshape(images, lat + patches, d)[:, patches:].reshape(images * lat, d)
    gg = gg.swapaxes(0, 1).reshape(images * lat, ff)
    dh = dh.swapaxes(0, 1).reshape(images * lat, ff)
    up_t = dot_tn(dh, nf).astype(BF16).reshape(dp, ff // dp, d)
    down_t = dot_tn(df, gg).astype(BF16).reshape(dp, d // dp * (ff // d), d)
    query_t = dot_tn(dq, nx).astype(BF16).reshape(dp, inner // dp, d)
    kv_t = dot_tn(dkv, kin).astype(BF16).reshape(2, dp, inner // dp, d)
    output_t = dot_tn(da, att).astype(BF16).reshape(dp, d // dp * inner // d, d)
    norm_t = norm_grads.astype(BF16).reshape(8, dp, d // dp).swapaxes(0, 1)
    norm_t = jnp.pad(norm_t.reshape(dp, 1, 8 * d // dp), ((0, 0), (0, 15), (0, d - 8 * d // dp)))
    packed = jnp.concatenate([up_t, down_t, query_t, kv_t[0], kv_t[1], output_t, norm_t], axis=1)
    summed = lax.psum_scatter(packed, "dp", scatter_dimension=0, tiled=False).astype(F32)
    sizes = [ff // dp, ff // dp, inner // dp, inner // dp, inner // dp, inner // dp]
    parts, at = [], 0
    for size in sizes:
        parts.append(summed[at : at + size])
        at += size
    norm_part = summed[at, : 8 * d // dp].reshape(8, d // dp)
    down_g = parts[1].reshape(d // dp, ff).T
    out_g = parts[5].reshape(d // dp, inner).T
    attn = [part.T for part in parts[2:5]]
    return came, med_came, attn, down_g, out_g, parts[0].T, norm_part


def local(
    latents,
    media_tokens,
    image_counts,
    cotangent,
    query_weight,
    key_weight,
    value_weight,
    output_weight,
    up_weight,
    down_weight,
    media_gain,
    media_bias,
    latent_gain,
    latent_bias,
    feed_gain,
    feed_bias,
):
    micro_count, samples, slot_count, lat, half = latents.shape
    patches = media_tokens.shape[3]
    images = micro_count * samples * slot_count
    d = 2 * half
    dp = lax.axis_size("dp")
    section = lax.axis_index("section")
    weights = (
        query_weight[0],
        key_weight[0],
        value_weight[0],
        output_weight[0],
        up_weight[0],
        down_weight[0],
    )
    norms = (media_gain, media_bias, latent_gain, latent_bias, feed_gain, feed_bias)
    inner, ff = query_weight.shape[2], up_weight.shape[2]
    gg, dh, nf, df, att, da, dq, kin, dkv, res, latgrad, dmed, norm_grads = run_layers(
        latents.reshape(images, lat, half),
        media_tokens.reshape(images, patches, half),
        cotangent.reshape(images, lat, half),
        image_counts.reshape(-1),
        weights,
        norms,
        slot_count,
    )
    lead = (micro_count, samples, slot_count)
    saved = (gg, dh, nf, df, att, da, dq, kin, dkv)
    fits = dp % 4 == 0 and ff // dp % 256 == 0 and half % (ff // dp // 2) == 0
    fits = fits and inner // dp % 16 == 0 and d // dp * inner % d == 0 and ff // d % 2 == 0
    if fits:
        main, attn_t, came, med_came = run_reduce(saved, norm_grads, res, latgrad, dmed, dp)
        outs = run_outputs(dmed, med_came, res, latgrad, came, main, attn_t, section, dp)
        resampled, latent_grad, media_grad, up_g, down_t, *parts = outs
        return (
            resampled.reshape(lead + (lat, half)),
            latent_grad.reshape(lead + (lat, half)),
            media_grad.reshape(lead + (patches, half)),
            parts[0].T[None],
            parts[1].T[None],
            parts[2].T[None],
            parts[3].T[None],
            up_g[None],
            down_t.T[None],
            *parts[4:],
        )
    came, med_came, parts, down_g, out_g, up_g, norm_part = plain_reduce(
        saved, norm_grads, res, latgrad, dmed, dp
    )
    resampled = jnp.where(section == 0, came, res[..., half:])
    latent_grad = jnp.where(section == 0, latgrad[..., :half], came).astype(F32)
    med_mine = lax.dynamic_index_in_dim(dmed, section, 0, keepdims=False)
    media_grad = med_mine.astype(F32) + med_came.astype(F32)
    return (
        resampled.reshape(lead + (lat, half)),
        latent_grad.reshape(lead + (lat, half)),
        media_grad.reshape(lead + (patches, half)),
        parts[0][None],
        parts[1][None],
        parts[2][None],
        out_g[None],
        up_g[None],
        down_g[None],
        *[norm_part[i][None] for i in range(6)],
    )


def solution(mesh):
    feature = P(None, "dp", None, None, "section")
    weight = P("section", None, None)
    vector = P("section", None)
    in_specs = (feature, feature, P(None, "dp"), feature) + (weight,) * 6 + (vector,) * 6
    out_specs = (feature,) * 3 + (P("section", None, "dp"),) * 6 + (P("section", "dp"),) * 6
    return jax.shard_map(
        local, mesh=mesh, in_specs=in_specs, out_specs=out_specs, check_vma=False
    )
```

```python
import functools

import jax
import jax.numpy as jnp
from jax import lax
from jax.experimental import pallas as pl
from jax.experimental.pallas import tpu as pltpu
from jax.sharding import PartitionSpec as P

DH = 64
EPS = 1e-05
QUERY_SCALE = 0.125
QUAD = 4
GROUP = 2
F32, BF16 = jnp.float32, jnp.bfloat16


def dot(a, b):
    return lax.dot_general(a, b, (((1,), (0,)), ((), ())), preferred_element_type=F32)


def dot_nt(a, b):
    return lax.dot_general(a, b, (((1,), (1,)), ((), ())), preferred_element_type=F32)


def dot_tn(a, b):
    return lax.dot_general(a, b, (((0,), (0,)), ((), ())), preferred_element_type=F32)


def standardize(rows):
    centered = rows - jnp.mean(rows, -1, keepdims=True)
    inverse = lax.rsqrt(jnp.mean(centered * centered, -1, keepdims=True) + EPS)
    return centered * inverse, inverse


def gelu_parts(hidden):
    t = 1.0 / (1.0 + (0.3275911 * 0.5**0.5) * jnp.abs(hidden))
    bell = jnp.exp(hidden * hidden * -0.5)
    series = 0.5 * 1.061405429
    for term in (-1.453152027, 1.421413741, -0.284496736, 0.254829592):
        series = series * t + 0.5 * term
    tail = series * t * bell
    below = jnp.where(hidden < 0.0, tail, 1.0 - tail)
    return hidden * below, below + hidden * bell * 0.3989422804014327


def norm_back(grads, standard, inverse, gain):
    scaled = grads * gain
    return inverse * (
        scaled
        - jnp.mean(scaled, -1, keepdims=True)
        - standard * jnp.mean(scaled * standard, -1, keepdims=True)
    )


def layers_kernel(
    dims,
    counts,
    media_gain,
    media_bias,
    latent_gain,
    latent_bias,
    feed_gain,
    feed_bias,
    latents,
    media,
    cotangent,
    wq_hbm,
    wk_hbm,
    wv_hbm,
    wo_hbm,
    up_hbm,
    down_hbm,
    gg_out,
    dh_out,
    nf_out,
    df_out,
    att_out,
    da_out,
    dq_out,
    kin_out,
    dkv_out,
    rows_out,
    latgrad_out,
    dmed_out,
    norm_grads,
    wq,
    wkv,
    wo,
    up,
    down,
    med_in,
    x_in,
    g_in,
    q_keep,
    kv_keep,
    pr_keep,
    x1_keep,
    slope_keep,
    y_stage,
    dy_stage,
    kin_st,
    gg_st,
    dh_st,
    nf_st,
    df_st,
    att_st,
    da_st,
    dq_st,
    dmed_st,
    acc,
    dkin,
    w_sem,
    own_sem,
    xown_sem,
    gown_sem,
    med_send,
    med_recv,
    x_send,
    x_recv,
    g_send,
    g_recv,
    f_sem,
    b_sem,
    m_sem,
    row_sem,
    lg_sem,
):
    images, patches, lat, d, inner, ff, slots = dims
    keys = patches + lat
    half = d // 2
    quads = inner // (QUAD * DH)
    qw = QUAD * DH
    size = GROUP if images % GROUP == 0 else 1
    steps = images // size
    sec = lax.axis_index("section")
    peer = 1 - sec
    first = sec == 0
    second = jnp.logical_not(first)
    mine = pl.ds(pl.multiple_of(sec * half, half), half)
    theirs = pl.ds(pl.multiple_of(peer * half, half), half)
    there = {"section": peer}

    def remote(src, dst, send, recv):
        return pltpu.make_async_remote_copy(
            src_ref=src,
            dst_ref=dst,
            send_sem=send,
            recv_sem=recv,
            device_id=there,
            device_id_type=pl.DeviceIdType.MESH,
        )

    def med_copy(n):
        return remote(media.at[n], med_in.at[n, :, mine], med_send.at[n], med_recv.at[n])

    def med_arrival(n):
        return remote(media.at[n], med_in.at[n, :, theirs], med_send.at[n], med_recv.at[n])

    def lat_copy(n, lanes):
        return remote(latents.at[n], x_in.at[n, :, lanes], x_send.at[n], x_recv.at[n])

    def cot_copy(n, lanes):
        return remote(cotangent.at[n], g_in.at[n, :, lanes], g_send.at[n], g_recv.at[n])

    def y_copy(n):
        return remote(y_stage.at[n], x_in.at[n], x_send.at[n], x_recv.at[n])

    def dy_copy(n):
        return remote(dy_stage.at[n], g_in.at[n], g_send.at[n], g_recv.at[n])

    def med_own(n):
        return pltpu.make_async_copy(media.at[n], med_in.at[n, :, mine], own_sem.at[n])

    lat_own = pltpu.make_async_copy(latents, x_in.at[:, :, mine], xown_sem)
    cot_own = pltpu.make_async_copy(cotangent, g_in.at[:, :, mine], gown_sem)

    weight_copies = [
        pltpu.make_async_copy(wk_hbm, wkv.at[:, pl.ds(0, inner)], w_sem.at[0]),
        pltpu.make_async_copy(wv_hbm, wkv.at[:, pl.ds(inner, inner)], w_sem.at[1]),
        pltpu.make_async_copy(wq_hbm, wq, w_sem.at[2]),
        pltpu.make_async_copy(wo_hbm, wo, w_sem.at[3]),
        pltpu.make_async_copy(up_hbm, up, w_sem.at[4]),
        pltpu.make_async_copy(down_hbm, down, w_sem.at[5]),
    ]

    barrier = pltpu.get_barrier_semaphore()
    pl.semaphore_signal(
        barrier, inc=1, device_id=there, device_id_type=pl.DeviceIdType.MESH
    )
    pl.semaphore_wait(barrier, 1)

    for n in range(images):
        med_own(n).start()

    early = min(4, images)

    @pl.when(first)
    def _():
        lat_own.start()
        for n in range(min(2, images)):
            med_copy(n).start()

    @pl.when(second)
    def _():
        cot_own.start()
        for n in range(min(2, images)):
            lat_copy(n, mine).start()
            med_copy(n).start()

    for copy in weight_copies:
        copy.start()
    norm_grads[...] = jnp.zeros_like(norm_grads)

    @pl.when(first)
    def _():
        lat_own.wait()
        for n in range(2, early):
            med_copy(n - 2).wait_send()
            med_copy(n).start()

    @pl.when(second)
    def _():
        cot_own.wait()
        for n in range(2, early):
            med_copy(n - 2).wait_send()
            lat_copy(n, mine).start()
            med_copy(n).start()

    def later_images(k, act):
        for i in range(2):
            n = early + 2 * k + i

            @pl.when(n < images)
            def _(n=n):
                act(n)

    def send_features(n):
        lat_copy(n, mine).start()
        med_copy(n).start()

    def lane_head(n, h):
        return (lax.broadcasted_iota(jnp.int32, (n, qw), 1) // DH) == h

    def spread(quad_rows):
        return jnp.concatenate(
            [
                jnp.where(lane_head(lat, h), quad_rows, jnp.zeros_like(quad_rows))
                for h in range(QUAD)
            ],
            axis=0,
        )

    def gather_heads(stacked):
        total = jnp.where(lane_head(lat, 0), stacked[:lat], 0.0)
        for h in range(1, QUAD):
            total = total + jnp.where(
                lane_head(lat, h), stacked[h * lat : (h + 1) * lat], 0.0
            )
        return total

    def f_copies(n, i):
        r, own = pl.ds(n * lat, lat), pl.ds(i * lat, lat)
        return [
            pltpu.make_async_copy(gg_st.at[:, own], gg_out.at[:, r], f_sem.at[4 * i]),
            pltpu.make_async_copy(nf_st.at[own], nf_out.at[r], f_sem.at[4 * i + 1]),
            pltpu.make_async_copy(att_st.at[own], att_out.at[r], f_sem.at[4 * i + 2]),
            pltpu.make_async_copy(
                kin_st.at[i], kin_out.at[pl.ds(n * keys, keys)], f_sem.at[4 * i + 3]
            ),
        ]

    def b_copies(n, i):
        r, own = pl.ds(n * lat, lat), pl.ds(i * lat, lat)
        return [
            pltpu.make_async_copy(dh_st.at[:, own], dh_out.at[:, r], b_sem.at[5 * i]),
            pltpu.make_async_copy(df_st.at[own], df_out.at[r], b_sem.at[5 * i + 1]),
            pltpu.make_async_copy(da_st.at[own], da_out.at[r], b_sem.at[5 * i + 2]),
            pltpu.make_async_copy(dq_st.at[own], dq_out.at[r], b_sem.at[5 * i + 3]),
            pltpu.make_async_copy(
                kv_keep.at[n], dkv_out.at[pl.ds(n * keys, keys)], b_sem.at[5 * i + 4]
            ),
        ]

    def m_copies(n, i):
        return [
            pltpu.make_async_copy(dmed_st.at[0, i], dmed_out.at[0, n], m_sem.at[2 * i]),
            pltpu.make_async_copy(dmed_st.at[1, i], dmed_out.at[1, n], m_sem.at[2 * i + 1]),
        ]

    def settle(copies, k, count):
        for i in range(count):

            @pl.when(k > 0)
            def _(i=i):
                for copy in copies(0, i):
                    copy.wait()

    def row_copy(n):
        return pltpu.make_async_copy(y_stage.at[n], rows_out.at[n], row_sem.at[n])

    def lg_copy(n):
        return pltpu.make_async_copy(dy_stage.at[n], latgrad_out.at[n], lg_sem.at[n])

    def mask_of(image):
        sample = image // slots
        return jnp.where(image - sample * slots < counts[sample], 1.0, 0.0)

    step_rows = 64
    ff_tile = d // 2
    tiles = ff // ff_tile

    def forward(k, start, count):
        rows = count * lat
        span = pl.ds(start, count)
        settle(f_copies, k, count)
        for i in range(count):
            med_own(start + i).wait()
            med_arrival(start + i).wait_recv()

        @pl.when(k == 0)
        def _():
            for copy in weight_copies[:4]:
                copy.wait()

        for i in range(count):
            for j in range(patches // step_rows):
                r = slice(j * step_rows, (j + 1) * step_rows)
                standard, _ = standardize(med_in[start + i, r, :].astype(F32))
                kin_st[i, r, :] = (standard * media_gain[...] + media_bias[...]).astype(BF16)

        n_tile = 512
        for i in range(count):
            for j in range(2 * inner // n_tile):
                cols = slice(j * n_tile, (j + 1) * n_tile)
                kv_keep[start + i, :patches, cols] = dot(
                    kin_st[i, :patches, :], wkv[:, cols]
                ).astype(BF16)

        @pl.when(first)
        def _():
            for i in range(count):
                lat_copy(start + i, theirs).wait_recv()

        @pl.when(second)
        def _():
            for i in range(count):
                y_copy(start + i).wait_recv()
            later_images(2 * k, send_features)

        x = x_in[span].reshape(rows, d).astype(F32)
        standard, _ = standardize(x)
        nx = (standard * latent_gain[...] + latent_bias[...]).astype(BF16)
        own_kv = dot(nx, wkv[...]).astype(BF16)
        for i in range(count):
            kin_st[i, patches:, :] = nx[i * lat : (i + 1) * lat]
            kv_keep[start + i, patches:, :] = own_kv[i * lat : (i + 1) * lat]
        q = (dot(nx, wq[...]) * QUERY_SCALE).astype(BF16)
        q_keep[span] = q.reshape(count, lat, inner)

        for i in range(count):
            for g in range(quads):
                lanes = slice(g * qw, (g + 1) * qw)
                stack = spread(q[i * lat : (i + 1) * lat, lanes])
                scores = dot_nt(stack, kv_keep[start + i, :, lanes])
                top = jnp.max(scores, -1, keepdims=True)
                powers = jnp.exp(scores - top)
                probs = (powers * (1.0 / jnp.sum(powers, -1, keepdims=True))).astype(BF16)
                pr_keep[start + i, g] = probs
                mixed = dot(probs, kv_keep[start + i, :, inner + g * qw : inner + (g + 1) * qw])
                att_st[i * lat : (i + 1) * lat, lanes] = gather_heads(mixed).astype(BF16)

        x1 = x + dot(att_st[:rows, :], wo[...])
        x1_keep[span] = x1.reshape(count, lat, d)
        standard, _ = standardize(x1)
        normed = (standard * feed_gain[...] + feed_bias[...]).astype(BF16)
        nf_st[:rows, :] = normed

        @pl.when(k == 0)
        def _():
            for copy in weight_copies[4:]:
                copy.wait()

        acc[:rows, :] = x1
        hidden = dot(normed, up[:, :ff_tile])
        for j in range(tiles):
            if j + 1 < tiles:
                ahead = dot(normed, up[:, (j + 1) * ff_tile : (j + 2) * ff_tile])
            active, slope = gelu_parts(hidden)
            slope_keep[span, :, j * ff_tile : (j + 1) * ff_tile] = slope.astype(BF16).reshape(
                count, lat, ff_tile
            )
            active = active.astype(BF16)
            gg_st[j, :rows, :] = active
            acc[:rows, :] += dot(active, down[j * ff_tile : (j + 1) * ff_tile, :])
            hidden = ahead

        for i in range(count):
            scale = jnp.where(first, 1.0, mask_of(start + i))
            y_stage[start + i] = (acc[i * lat : (i + 1) * lat, :] * scale).astype(BF16)

        @pl.when(first)
        def _():
            for i in range(count):
                y_copy(start + i).start()
            for i in range(count):
                cot_copy(start + i, mine).start()
            later_images(k, lambda n: med_copy(n).start())

        @pl.when(second)
        def _():
            for i in range(count):
                row_copy(start + i).start()

        for i in range(count):
            for copy in f_copies(start + i, i):
                copy.start()

    def backward(k, start, count):
        rows = count * lat
        span = pl.ds(start, count)
        settle(b_copies, k, count)

        @pl.when(first)
        def _():
            for i in range(count):
                dy_copy(start + i).wait_recv()

        @pl.when(second)
        def _():
            later_images(2 * k + 1, send_features)
            for i in range(count):
                cot_copy(start + i, theirs).wait_recv()

        for i in range(count):
            scale = jnp.where(first, 1.0, mask_of(start + i))
            df_st[i * lat : (i + 1) * lat, :] = (
                g_in[start + i].astype(F32) * scale
            ).astype(BF16)
        grads_low = df_st[:rows, :]
        dg = dot_nt(grads_low, down[:ff_tile, :])
        for j in range(tiles):
            if j + 1 < tiles:
                ahead = dot_nt(grads_low, down[(j + 1) * ff_tile : (j + 2) * ff_tile, :])
            slope = slope_keep[span, :, j * ff_tile : (j + 1) * ff_tile]
            dh = (dg * slope.reshape(rows, ff_tile).astype(F32)).astype(BF16)
            dh_st[j, :rows, :] = dh
            more = dot_nt(dh, up[:, j * ff_tile : (j + 1) * ff_tile])
            acc[:rows, :] = more if j == 0 else acc[:rows, :] + more
            dg = ahead
        standard, inverse = standardize(x1_keep[span].reshape(rows, d))
        dnf = acc[:rows, :]
        norm_grads[4:5, :] += jnp.sum(dnf * standard, axis=0, keepdims=True)
        norm_grads[5:6, :] += jnp.sum(dnf, axis=0, keepdims=True)
        dx1 = grads_low.astype(F32) + norm_back(dnf, standard, inverse, feed_gain[...])
        acc[:rows, :] = dx1
        da = dx1.astype(BF16)
        da_st[:rows, :] = da
        datt = dot_nt(da, wo[...]).astype(BF16)
        for i in range(count):
            for g in range(quads):
                lanes = slice(g * qw, (g + 1) * qw)
                vlanes = slice(inner + g * qw, inner + (g + 1) * qw)
                lr = slice(i * lat, (i + 1) * lat)
                stack = spread(datt[lr, lanes])
                dp = dot_nt(stack, kv_keep[start + i, :, vlanes])
                probs = pr_keep[start + i, g]
                wide = probs.astype(F32)
                ds = (wide * (dp - jnp.sum(wide * dp, -1, keepdims=True))).astype(BF16)
                mixed = gather_heads(dot(ds, kv_keep[start + i, :, lanes])).astype(BF16)
                dq_st[lr, lanes] = (mixed.astype(F32) * QUERY_SCALE).astype(BF16)
                dvv = dot_tn(probs, stack).astype(BF16)
                dkk = dot_tn(ds, spread(q_keep[start + i, :, lanes])).astype(BF16)
                kv_keep[start + i, :, vlanes] = dvv
                kv_keep[start + i, :, lanes] = dkk

        d_lat = jnp.concatenate([kv_keep[start + i, patches:, :] for i in range(count)], axis=0)
        dnx = dot_nt(d_lat, wkv[...]) + dot_nt(dq_st[:rows, :], wq[...])
        standard, inverse = standardize(x_in[span].reshape(rows, d).astype(F32))
        norm_grads[2:3, :] += jnp.sum(dnx * standard, axis=0, keepdims=True)
        norm_grads[3:4, :] += jnp.sum(dnx, axis=0, keepdims=True)
        dx = acc[:rows, :] + norm_back(dnx, standard, inverse, latent_gain[...])
        dy_stage[span] = dx.astype(BF16).reshape(count, lat, d)

        @pl.when(first)
        def _():
            for i in range(count):
                lg_copy(start + i).start()

        @pl.when(second)
        def _():
            for i in range(count):
                dy_copy(start + i).start()

        for i in range(count):
            for copy in b_copies(start + i, i):
                copy.start()

    def media_part(n):
        slot = n - n // 2 * 2

        @pl.when(n > 1)
        def _():
            for copy in m_copies(0, slot):
                copy.wait()

        dkin[...] = dot_nt(kv_keep[n, :patches, :], wkv[...])
        for j in range(patches // step_rows):
            r = slice(j * step_rows, (j + 1) * step_rows)
            standard, inverse = standardize(med_in[n, r, :].astype(F32))
            grads = dkin[r, :]
            norm_grads[0:1, :] += jnp.sum(grads * standard, axis=0, keepdims=True)
            norm_grads[1:2, :] += jnp.sum(grads, axis=0, keepdims=True)
            out = norm_back(grads, standard, inverse, media_gain[...]).astype(BF16)
            dmed_st[0, slot, r, :] = out[:, :half]
            dmed_st[1, slot, r, :] = out[:, half:]
        for copy in m_copies(n, slot):
            copy.start()

    lead = max(steps - 1, 1)
    order_first = [(0, k) for k in range(lead)] + [(1, 0)] + [(0, k) for k in range(lead, steps)]
    waiting = [0]
    for k in range(1, steps):
        order_first.append((1, k))
        waiting.append(k)
        while len(waiting) > (1 if k < steps - 2 else 0):
            order_first.append((2, waiting.pop(0)))
    order_first += [(2, k) for k in waiting]
    order_second = [(kind, k) for k in range(steps) for kind in (0, 1)]
    order_second += [(2, k) for k in range(steps)]
    assert sorted(order_first) == sorted(order_second)

    def chosen_of(t, field):
        value = jnp.int32(0)
        for n, (a, b) in enumerate(zip(order_first, order_second)):
            value = jnp.where(t == n, jnp.where(first, a[field], b[field]), value)
        return value

    def step(t, carry):
        kind, k = chosen_of(t, 0), chosen_of(t, 1)
        start = k * size

        @pl.when(kind == 0)
        def _():
            forward(k, start, size)

        @pl.when(kind == 1)
        def _():
            backward(k, start, size)

        @pl.when(kind == 2)
        def _():
            def body(i, carry):
                media_part(start + i)
                return carry

            lax.fori_loop(0, size, body, 0)

        return carry

    lax.fori_loop(0, 3 * steps, step, 0)

    for i in range(size):
        for copy in f_copies(0, i) + b_copies(0, i):
            copy.wait()
    for i in range(min(2, images)):
        for copy in m_copies(0, i):
            copy.wait()

    for n in range(early - 2, images):
        med_copy(n).wait_send()

    @pl.when(first)
    def _():
        for n in range(images):
            lg_copy(n).wait()
            y_copy(n).wait_send()
            cot_copy(n, mine).wait_send()

    @pl.when(second)
    def _():
        for n in range(images):
            row_copy(n).wait()
            lat_copy(n, mine).wait_send()
            dy_copy(n).wait_send()


def run_layers(latents, media, cotangent, counts, weights, norms, slots):
    images, lat, half = latents.shape
    patches = media.shape[1]
    d = 2 * half
    wq, wk, wv, wo, up, down = weights
    inner, ff = wq.shape[1], up.shape[1]
    keys = patches + lat
    rows = GROUP * lat
    quads = inner // (QUAD * DH)
    dims = (images, patches, lat, d, inner, ff, slots)
    total, wide = images * lat, images * keys

    def out(*shape, dtype=BF16):
        return jax.ShapeDtypeStruct(shape, dtype)

    any_spec = pl.BlockSpec(memory_space=pl.ANY)
    vmem_spec = pl.BlockSpec(memory_space=pltpu.VMEM)
    dma = pltpu.SemaphoreType.DMA
    return pl.pallas_call(
        functools.partial(layers_kernel, dims),
        out_shape=(
            out(2 * ff // d, total, half),
            out(2 * ff // d, total, half),
            out(total, d),
            out(total, d),
            out(total, inner),
            out(total, d),
            out(total, inner),
            out(wide, d),
            out(wide, 2 * inner),
            out(images, lat, d),
            out(images, lat, d),
            out(2, images, patches, half),
            out(8, d, dtype=F32),
        ),
        in_specs=[pl.BlockSpec(memory_space=pltpu.SMEM)] + [vmem_spec] * 6 + [any_spec] * 9,
        out_specs=(any_spec,) * 12 + (vmem_spec,),
        scratch_shapes=[
            pltpu.VMEM((d, inner), BF16),
            pltpu.VMEM((d, 2 * inner), BF16),
            pltpu.VMEM((inner, d), BF16),
            pltpu.VMEM((d, ff), BF16),
            pltpu.VMEM((ff, d), BF16),
            pltpu.VMEM((images, patches, d), BF16),
            pltpu.VMEM((images, lat, d), BF16),
            pltpu.VMEM((images, lat, d), BF16),
            pltpu.VMEM((images, lat, inner), BF16),
            pltpu.VMEM((images, keys, 2 * inner), BF16),
            pltpu.VMEM((images, quads, QUAD * lat, keys), BF16),
            pltpu.VMEM((images, lat, d), F32),
            pltpu.VMEM((images, lat, ff), BF16),
            pltpu.VMEM((images, lat, d), BF16),
            pltpu.VMEM((images, lat, d), BF16),
            pltpu.VMEM((GROUP, keys, d), BF16),
            pltpu.VMEM((2 * ff // d, rows, half), BF16),
            pltpu.VMEM((2 * ff // d, rows, half), BF16),
            pltpu.VMEM((rows, d), BF16),
            pltpu.VMEM((rows, d), BF16),
            pltpu.VMEM((rows, inner), BF16),
            pltpu.VMEM((rows, d), BF16),
            pltpu.VMEM((rows, inner), BF16),
            pltpu.VMEM((2, 2, patches, half), BF16),
            pltpu.VMEM((rows, d), F32),
            pltpu.VMEM((patches, d), F32),
            dma((6,)),
            dma((images,)),
            dma,
            dma,
            dma((images,)),
            dma((images,)),
            dma((images,)),
            dma((images,)),
            dma((images,)),
            dma((images,)),
            dma((4 * GROUP,)),
            dma((5 * GROUP,)),
            dma((4,)),
            dma((images,)),
            dma((images,)),
        ],
        compiler_params=pltpu.CompilerParams(
            collective_id=0, has_side_effects=True, vmem_limit_bytes=63 * 2**20
        ),
        cost_estimate=pl.CostEstimate(
            flops=4 * images * 960_000_000, bytes_accessed=80_000_000, transcendentals=0
        ),
        name="layers",
    )(counts, *norms, latents, media, cotangent, wq, wk, wv, wo, up, down)


def reduce_kernel(
    dims,
    norm_grads,
    gg,
    dh,
    nf,
    df,
    att,
    da,
    dq,
    kin,
    dkv,
    rows_in,
    latgrad,
    dmed,
    main_out,
    attn_out,
    came,
    med_came,
    g_up1,
    g_up0,
    g_down0,
    g_low,
    g_high,
    g_attn,
    core_slots,
    x_up1,
    x_up0,
    x_down0,
    x_low,
    x_high,
    x_attn,
    z_up1,
    z_up0,
    z_down0,
    z_low,
    z_high,
    z_attn,
    buf_a,
    buf_b,
    flipped,
    att_v,
    dq_v,
    big_a,
    dh_v,
    big_b,
    stage,
    attn_stage,
    load_sem,
    core_send,
    core_recv,
    x_send,
    x_recv,
    zr_send,
    zr_recv,
    zl_send,
    zl_recv,
    y_send,
    y_recv,
    credit,
    main_sem,
    attn_sem,
):
    images, lat, patches, d, inner, ff, dp = dims
    line = dp // 4
    keys = lat + patches
    total = images * lat
    block = ff // dp // 2
    half = d // 2
    blocks = ff // half
    me = lax.axis_index("dp")
    sec = lax.axis_index("section")
    z = me // 4
    x = me // 2 - z * 2
    c = me - (me // 2) * 2
    sibling = {"dp": me + 1 - 2 * c}
    across = {"dp": me + 2 - 4 * x}
    ahead = {"dp": jnp.minimum(me + 4, dp - 4 + (me - z * 4))}
    behind = {"dp": jnp.maximum(me - 4, me - z * 4)}
    peer = {"section": 1 - sec}
    has_left, has_right = z > 0, z < line - 1
    mesh_ids = pl.DeviceIdType.MESH

    def place(dest):
        return dest % 2, (dest // 2) % 2, dest // 4

    def remote(src, dst, send, recv, device):
        return pltpu.make_async_remote_copy(
            src_ref=src,
            dst_ref=dst,
            send_sem=send,
            recv_sem=recv,
            device_id=device,
            device_id_type=mesh_ids,
        )

    barrier = pltpu.get_barrier_semaphore()
    for device in (sibling, across, peer):
        pl.semaphore_signal(barrier, inc=1, device_id=device, device_id_type=mesh_ids)

    @pl.when(has_left)
    def _():
        pl.semaphore_signal(barrier, inc=1, device_id=behind, device_id_type=mesh_ids)

    @pl.when(has_right)
    def _():
        pl.semaphore_signal(barrier, inc=1, device_id=ahead, device_id_type=mesh_ids)

    def load(src, dst, k):
        return pltpu.make_async_copy(src, dst, load_sem.at[k])

    part = pl.ds(0, images * keys)
    loads = {
        "nf": load(nf, buf_a, 0),
        "dh": load(dh, dh_v, 1),
        "df": load(df, buf_b, 2),
        "gg": load(gg, big_b, 3),
        "att": load(att, att_v, 4),
        "dq": load(dq, dq_v, 5),
        "da": load(da, buf_a, 6),
        "kin": load(kin, big_a, 7),
        "dk": load(dkv.at[:, pl.ds(0, inner)], big_b.at[part], 8),
        "dv": load(dkv.at[:, pl.ds(inner, inner)], big_b.at[part], 9 + images),
    }
    nx_loads = [
        load(kin.at[pl.ds(i * keys + patches, lat)], buf_b.at[pl.ds(i * lat, lat)], 9 + i)
        for i in range(images)
    ]
    for name in ("nf", "dh"):
        loads[name].start()

    pl.semaphore_wait(
        barrier, 3 + jnp.where(has_left, 1, 0) + jnp.where(has_right, 1, 0)
    )

    def out_rows(src, lanes):
        return remote(src.at[:, :, lanes], came, y_send.at[0], y_recv.at[0], peer)

    out_first = out_rows(latgrad, pl.ds(half, half))
    out_second = out_rows(rows_in, pl.ds(0, half))
    out_media = remote(dmed.at[1 - sec], med_came, y_send.at[1], y_recv.at[1], peer)

    @pl.when(sec == 0)
    def _():
        out_first.start()

    @pl.when(sec == 1)
    def _():
        out_second.start()

    out_media.start()

    grads = [g_up1, g_up0, g_down0, g_low, g_high, g_attn]
    count = len(grads)
    core_in = [
        core_slots.at[n % 2, :, :, pl.ds(0, grads[n].shape[3])] for n in range(count)
    ]
    x_in = [x_up1, x_up0, x_down0, x_low, x_high, x_attn]
    z_in = [z_up1, z_up0, z_down0, z_low, z_high, z_attn]
    z_first = 0

    def up_piece(h):
        wide = ff // dp
        groups = half // block
        for j in range(blocks):
            tile = dot(
                flipped[h * half : (h + 1) * half, :], dh_v[j * total : (j + 1) * total, :]
            ).astype(BF16)
            for i in range(half // wide):
                pc, px, pz = place(j * (half // wide) + i)
                for k in range(groups):
                    grads[1 - h][pc, px, pz, :, k * wide : (k + 1) * wide] = tile[
                        k * block : (k + 1) * block, i * wide : (i + 1) * wide
                    ]

    def down_piece(p):
        own = d // dp
        tiles = range(blocks // 2) if p == 2 else range(blocks // 4)
        start = 0 if p == 2 else (p - 1) * (blocks // 4)
        for k in tiles:
            j = start + k
            at = k * half
            r = slice(at // d * own, at // d * own + own)
            lanes = slice(at % d, at % d + half)
            for m in range(2):
                tile = dot(
                    flipped[m * half : (m + 1) * half, :], big_b[j * total : (j + 1) * total, :]
                ).astype(BF16)
                for i in range(half // own):
                    pc, px, pz = place(m * (half // own) + i)
                    grads[p][pc, px, pz, r, lanes] = tile[i * own : (i + 1) * own, :]

    def attn_piece():
        own = inner // dp
        lo = inner // 2

        def store(n, make):
            for m in range(2):
                tile = make(slice(m * lo, (m + 1) * lo)).astype(BF16)
                for i in range(lo // own):
                    pc, px, pz = place(m * (lo // own) + i)
                    g_attn[pc, px, pz, n * own : (n + 1) * own, :] = tile[
                        i * own : (i + 1) * own, :
                    ]

        for copy in nx_loads:
            copy.wait()
        store(0, lambda m: dot_tn(dq_v[:, m], buf_b[...]))
        loads["kin"].wait()
        loads["dk"].wait()
        store(1, lambda m: dot_tn(big_b[: images * keys, m], big_a[...]))
        loads["dv"].start()
        loads["dv"].wait()
        store(2, lambda m: dot_tn(big_b[: images * keys, m], big_a[...]))
        loads["da"].wait()
        out_own = d // dp
        for m in range(2):
            tile = dot_tn(buf_a[:, m * half : (m + 1) * half], att_v[...]).astype(BF16)
            for i in range(half // out_own):
                pc, px, pz = place(m * (half // out_own) + i)
                rest = tile[i * out_own : (i + 1) * out_own, :]
                g_attn[pc, px, pz, 3 * own : 4 * own, :inner] = rest[:own]
                g_attn[pc, px, pz, 3 * own : 4 * own, inner:] = rest[own:]
        lanes = 128
        for dest in range(dp):
            pc, px, pz = place(dest)
            at = (dest * (d // dp)) // lanes * lanes
            sums = norm_grads[:, at : at + lanes]
            g_attn[pc, px, pz, 4 * own :, :] = jnp.zeros((16, d), BF16)
            g_attn[pc, px, pz, 4 * own :, :lanes] = jnp.concatenate(
                [sums, jnp.zeros_like(sums)], axis=0
            ).astype(BF16)

    def core_copy(p):
        return remote(grads[p].at[1 - c], core_in[p], core_send.at[p], core_recv.at[p], sibling)

    def x_copy(p):
        if p == z_first:
            src = grads[p].at[c, 1 - x, z]
        else:
            src = grads[p].at[c, 1 - x]
        return remote(src, x_in[p], x_send.at[p], x_recv.at[p], across)

    def spot(p, t):
        if p == z_first:
            return grads[p].at[c, :, t]
        return grads[p].at[c, x, t]

    def right_copy(p, t):
        k = p * line + t
        return remote(spot(p, t), z_in[p].at[t + 1], zr_send.at[k], zr_recv.at[k], ahead)

    def left_copy(p, t):
        k = p * line + t
        return remote(spot(p, t), z_in[p].at[t], zl_send.at[k], zl_recv.at[k], behind)

    def add_into(target, source):
        target[...] = (target[...].astype(F32) + source[...].astype(F32)).astype(BF16)

    def core_add(p):
        core_copy(p).wait_recv()

        def body(n, carry):
            xx = n // line
            zz = n - xx * line
            add_into(grads[p].at[c, xx, zz], core_in[p].at[xx, zz])
            return carry

        lax.fori_loop(0, 2 * line, body, 0)

    def x_add(p):
        x_copy(p).wait_recv()

        def body(zz, carry):
            add_into(grads[p].at[c, x, zz], x_in[p].at[zz])
            return carry

        lax.fori_loop(0, line, body, 0)

    def z_ends(p):
        @pl.when(z == 0)
        def _():
            for t in range(line - 1, 0, -1):
                right_copy(p, t).start()

        @pl.when(z == line - 1)
        def _():
            for t in range(line - 1):
                left_copy(p, t).start()

    def z_phase(p, k):
        t = line - 1 - k

        def forward_right():
            @pl.when(has_left & (z < t))
            def _():
                right_copy(p, t).wait_recv()
                add_into(spot(p, t), z_in[p].at[t + 1])
                right_copy(p, t).start()

        def forward_left():
            @pl.when(has_right & (z > k))
            def _():
                left_copy(p, k).wait_recv()
                add_into(spot(p, k), z_in[p].at[k])
                left_copy(p, k).start()

        @pl.when(z < line // 2)
        def _():
            forward_right()
            forward_left()

        @pl.when(z >= line // 2)
        def _():
            forward_left()
            forward_right()

    def z_own(p):
        @pl.when(has_left)
        def _():
            for t in range(1, line):

                @pl.when(z == t)
                def _():
                    right_copy(p, t).wait_recv()
                    add_into(spot(p, t), z_in[p].at[t + 1])

        @pl.when(has_right)
        def _():
            for t in range(line - 1):

                @pl.when(z == t)
                def _():
                    left_copy(p, t).wait_recv()
                    add_into(spot(p, t), z_in[p].at[t])

    rows_of = [(block, block), (0, block), (2 * block, block), (3 * block, block // 2)]
    rows_of.append((3 * block + block // 2, block // 2))

    def main_copy(p):
        at, tall = rows_of[p]
        return pltpu.make_async_copy(
            stage.at[pl.ds(0, tall)], main_out.at[pl.ds(at, tall)], main_sem.at[p]
        )

    attn_copy = pltpu.make_async_copy(attn_stage, attn_out, attn_sem)
    staged = []

    def finish(p):
        result = grads[p].at[c, x, z][...].astype(F32)
        if p == z_first:
            result = result + x_in[p][...].astype(F32)
        if p == count - 1:
            attn_stage[...] = result
            attn_copy.start()
        else:
            if staged:
                main_copy(staged.pop()).wait()
            stage[: rows_of[p][1], :] = result
            main_copy(p).start()
            staged.append(p)

    def give_credit():
        pl.semaphore_signal(credit, inc=1, device_id=sibling, device_id_type=mesh_ids)

    loads["nf"].wait()
    flipped[...] = buf_a[...].T
    loads["da"].start()
    loads["dh"].wait()
    for name in ("df", "gg", "att", "dq", "kin"):
        loads[name].start()
    up_piece(1)
    core_copy(0).start()
    up_piece(0)
    core_copy(1).start()
    core_add(0)
    give_credit()
    z_ends(0)
    loads["df"].wait()
    flipped[...] = buf_b[...].T
    for copy in nx_loads:
        copy.start()
    loads["gg"].wait()
    core_add(1)
    give_credit()
    x_copy(1).start()
    down_piece(2)
    pl.semaphore_wait(credit, 1)
    core_copy(2).start()
    down_piece(3)
    pl.semaphore_wait(credit, 1)
    core_copy(3).start()
    core_add(2)
    give_credit()
    x_copy(2).start()
    z_phase(0, 0)
    down_piece(4)
    pl.semaphore_wait(credit, 1)
    core_copy(4).start()
    loads["dk"].start()
    core_add(3)
    give_credit()
    for k in range(1, line - 1):
        z_phase(0, k)
    loads["att"].wait()
    loads["dq"].wait()
    attn_piece()
    pl.semaphore_wait(credit, 1)
    core_copy(5).start()
    core_add(4)
    z_own(0)
    x_copy(0).start()
    core_add(5)
    order = [1, 2, 5, 3, 4]
    for n, p in enumerate(order):
        x_add(p)
        if n + 2 < len(order):
            x_copy(order[n + 2]).start()
        z_ends(p)
        if n > 0:
            z_own(order[n - 1])
            finish(order[n - 1])
        for k in range(line - 1):
            z_phase(p, k)
        if n == 1:
            x_copy(0).wait_recv()
            finish(0)
    z_own(order[-1])
    finish(order[-1])
    main_copy(staged.pop()).wait()
    attn_copy.wait()

    for p in range(count):
        core_copy(p).wait_send()
        x_copy(p).wait_send()
        for t in range(1, line):

            @pl.when(z < t)
            def _(p=p, t=t):
                right_copy(p, t).wait_send()

        for t in range(line - 1):

            @pl.when(z > t)
            def _(p=p, t=t):
                left_copy(p, t).wait_send()

    @pl.when(sec == 0)
    def _():
        out_first.wait()

    @pl.when(sec == 1)
    def _():
        out_second.wait()

    out_media.wait()


def run_reduce(saved, norm_grads, res, latgrad, dmed, dp):
    gg, dh, nf, df, att, da, dq, kin, dkv = saved
    images, lat, d = res.shape
    patches, half = dmed.shape[2:]
    inner, ff = att.shape[1], gg.shape[0] * half
    line = dp // 4
    block = ff // dp // 2
    tall = 4 * inner // dp + 16
    dims = (images, lat, patches, d, inner, ff, dp)
    total, wide = images * lat, images * (lat + patches)
    any_spec = pl.BlockSpec(memory_space=pl.ANY)
    vmem_spec = pl.BlockSpec(memory_space=pltpu.VMEM)
    dma = pltpu.SemaphoreType.DMA
    heights = (block, block, block, block // 2, block // 2, tall)
    pieces = len(heights)

    def low(*shape):
        return pltpu.VMEM(shape, BF16)

    return pl.pallas_call(
        functools.partial(reduce_kernel, dims),
        out_shape=(
            jax.ShapeDtypeStruct((4 * block, d), F32),
            jax.ShapeDtypeStruct((tall, d), F32),
            jax.ShapeDtypeStruct((images, lat, half), BF16),
            jax.ShapeDtypeStruct((images, patches, half), BF16),
        ),
        in_specs=[vmem_spec] + [any_spec] * 12,
        out_specs=(any_spec,) * 4,
        scratch_shapes=[
            *[low(2, 2, line, n, d) for n in heights],
            low(2, 2, line, tall, d),
            low(block, d),
            *[low(line, n, d) for n in heights[1:]],
            low(line + 1, 2, block, d),
            *[low(line + 1, n, d) for n in heights[1:]],
            low(total, d),
            low(total, d),
            low(d, total),
            low(total, inner),
            low(total, inner),
            low(wide, d),
            low(2 * ff // d * total, half),
            low(2 * ff // d * total, half),
            pltpu.VMEM((block, d), F32),
            pltpu.VMEM((tall, d), F32),
            dma((10 + images,)),
            dma((pieces,)),
            dma((pieces,)),
            dma((pieces,)),
            dma((pieces,)),
            dma((pieces * line,)),
            dma((pieces * line,)),
            dma((pieces * line,)),
            dma((pieces * line,)),
            dma((2,)),
            dma((2,)),
            pltpu.SemaphoreType.REGULAR,
            dma((pieces - 1,)),
            dma,
        ],
        compiler_params=pltpu.CompilerParams(
            collective_id=1, has_side_effects=True, vmem_limit_bytes=63 * 2**20
        ),
        cost_estimate=pl.CostEstimate(
            flops=2 * images * 960_000_000, bytes_accessed=60_000_000, transcendentals=0
        ),
        name="reduce",
    )(
        norm_grads,
        gg.reshape(-1, half),
        dh.reshape(-1, half),
        nf,
        df,
        att,
        da,
        dq,
        kin,
        dkv,
        res,
        latgrad,
        dmed,
    )


def outputs_kernel(
    dims,
    where,
    media_own,
    media_came,
    rows_in,
    latgrad,
    came,
    main,
    attn,
    resampled,
    latent_grad,
    media_grad,
    up_out,
    down_out,
    query_out,
    key_out,
    value_out,
    output_out,
    *norm_outs,
):
    block, share, own, inner, d, ff, dp = dims
    first = where[0] == 0
    media_grad[...] = media_own[0].astype(F32) + media_came[...].astype(F32)
    resampled[...] = jnp.where(first, came[...], rows_in[...])
    latent_grad[...] = jnp.where(first, latgrad[...], came[...]).astype(F32)

    @pl.when(pl.program_id(0) == 0)
    def _():
        half, wide = d // 2, ff // dp
        for h in range(2):
            for k in range(half // block):
                at = h * half + k * block
                up_out[at : at + block, :] = main[
                    h * block : (h + 1) * block, k * wide : (k + 1) * wide
                ]
        for k in range(ff // d):
            down_out[:, k * d : (k + 1) * d] = main[
                2 * block + k * share : 2 * block + (k + 1) * share, :
            ]
        query_out[...] = attn[:own, :]
        key_out[...] = attn[own : 2 * own, :]
        value_out[...] = attn[2 * own : 3 * own, :]
        output_out[:own, :] = attn[3 * own : 4 * own, :inner]
        output_out[own:, :] = attn[3 * own : 4 * own, inner:]
        sums = attn[4 * own : 4 * own + 8, :128]
        part = sums[:, :share]
        for n in range(1, 128 // share):
            part = jnp.where(where[1] == n, sums[:, n * share : (n + 1) * share], part)
        for n, out in enumerate(norm_outs):
            out[...] = part[n : n + 1, :]


def run_outputs(dmed, med_came, res, latgrad, came, main, attn, section, dp):
    images, lat, d = res.shape
    patches, half = dmed.shape[2:]
    several = 2 if images % 2 == 0 else 1
    block = main.shape[0] // 4
    ff = 2 * block * dp
    share = d // dp
    own = (attn.shape[0] - 16) // 4
    inner = own * dp
    place = jnp.stack([section, lax.axis_index("dp") % (128 // share)]).astype(jnp.int32)

    def whole(*shape):
        return pl.BlockSpec(shape, lambda n, w: (0,) * len(shape))

    def part(rows, lanes=0):
        return pl.BlockSpec((several, rows, half), lambda n, w: (n, 0, lanes))

    small = [(d, ff // dp), (share, ff), (own, d), (own, d), (own, d), (share, inner)]
    small += [(1, share)] * 6
    return pl.pallas_call(
        functools.partial(outputs_kernel, (block, share, own, inner, d, ff, dp)),
        out_shape=[
            jax.ShapeDtypeStruct((images, lat, half), BF16),
            jax.ShapeDtypeStruct((images, lat, half), F32),
            jax.ShapeDtypeStruct((images, patches, half), F32),
        ]
        + [jax.ShapeDtypeStruct(shape, F32) for shape in small],
        grid_spec=pltpu.PrefetchScalarGridSpec(
            num_scalar_prefetch=1,
            grid=(images // several,),
            in_specs=[
                pl.BlockSpec((1, several, patches, half), lambda n, w: (w[0], n, 0, 0)),
                part(patches),
                part(lat, 1),
                part(lat, 0),
                part(lat),
                whole(*main.shape),
                whole(*attn.shape),
            ],
            out_specs=[part(lat), part(lat), part(patches)] + [whole(*shape) for shape in small],
        ),
        compiler_params=pltpu.CompilerParams(vmem_limit_bytes=62 * 2**20),
        name="outputs",
    )(place, dmed, med_came, res, latgrad, came, main, attn)


def plain_reduce(saved, norm_grads, res, latgrad, dmed, dp):
    gg, dh, nf, df, att, da, dq, kin, dkv = saved
    images, lat, d = res.shape
    patches, half = dmed.shape[2:]
    inner, ff = att.shape[1], gg.shape[0] * half
    section = lax.axis_index("section")
    swap = [(0, 1), (1, 0)]
    to_send = jnp.where(section == 0, latgrad[..., half:], res[..., :half])
    came = lax.ppermute(to_send, "section", swap)
    med_theirs = lax.dynamic_index_in_dim(dmed, 1 - section, 0, keepdims=False)
    med_came = lax.ppermute(med_theirs, "section", swap)
    nx = kin.reshape(images, lat + patches, d)[:, patches:].reshape(images * lat, d)
    gg = gg.swapaxes(0, 1).reshape(images * lat, ff)
    dh = dh.swapaxes(0, 1).reshape(images * lat, ff)
    up_t = dot_tn(dh, nf).astype(BF16).reshape(dp, ff // dp, d)
    down_t = dot_tn(df, gg).astype(BF16).reshape(dp, d // dp * (ff // d), d)
    query_t = dot_tn(dq, nx).astype(BF16).reshape(dp, inner // dp, d)
    kv_t = dot_tn(dkv, kin).astype(BF16).reshape(2, dp, inner // dp, d)
    output_t = dot_tn(da, att).astype(BF16).reshape(dp, d // dp * inner // d, d)
    norm_t = norm_grads.astype(BF16).reshape(8, dp, d // dp).swapaxes(0, 1)
    norm_t = jnp.pad(norm_t.reshape(dp, 1, 8 * d // dp), ((0, 0), (0, 15), (0, d - 8 * d // dp)))
    packed = jnp.concatenate([up_t, down_t, query_t, kv_t[0], kv_t[1], output_t, norm_t], axis=1)
    summed = lax.psum_scatter(packed, "dp", scatter_dimension=0, tiled=False).astype(F32)
    sizes = [ff // dp, ff // dp, inner // dp, inner // dp, inner // dp, inner // dp]
    parts, at = [], 0
    for size in sizes:
        parts.append(summed[at : at + size])
        at += size
    norm_part = summed[at, : 8 * d // dp].reshape(8, d // dp)
    down_g = parts[1].reshape(d // dp, ff).T
    out_g = parts[5].reshape(d // dp, inner).T
    attn = [part.T for part in parts[2:5]]
    return came, med_came, attn, down_g, out_g, parts[0].T, norm_part


def local(
    latents,
    media_tokens,
    image_counts,
    cotangent,
    query_weight,
    key_weight,
    value_weight,
    output_weight,
    up_weight,
    down_weight,
    media_gain,
    media_bias,
    latent_gain,
    latent_bias,
    feed_gain,
    feed_bias,
):
    micro_count, samples, slot_count, lat, half = latents.shape
    patches = media_tokens.shape[3]
    images = micro_count * samples * slot_count
    d = 2 * half
    dp = lax.axis_size("dp")
    section = lax.axis_index("section")
    weights = (
        query_weight[0],
        key_weight[0],
        value_weight[0],
        output_weight[0],
        up_weight[0],
        down_weight[0],
    )
    norms = (media_gain, media_bias, latent_gain, latent_bias, feed_gain, feed_bias)
    inner, ff = query_weight.shape[2], up_weight.shape[2]
    gg, dh, nf, df, att, da, dq, kin, dkv, res, latgrad, dmed, norm_grads = run_layers(
        latents.reshape(images, lat, half),
        media_tokens.reshape(images, patches, half),
        cotangent.reshape(images, lat, half),
        image_counts.reshape(-1),
        weights,
        norms,
        slot_count,
    )
    lead = (micro_count, samples, slot_count)
    saved = (gg, dh, nf, df, att, da, dq, kin, dkv)
    fits = dp % 4 == 0 and ff // dp % 256 == 0 and half % (ff // dp // 2) == 0
    fits = fits and inner // dp % 16 == 0 and d // dp * inner % d == 0 and ff // d % 2 == 0
    if fits:
        main, attn_t, came, med_came = run_reduce(saved, norm_grads, res, latgrad, dmed, dp)
        outs = run_outputs(dmed, med_came, res, latgrad, came, main, attn_t, section, dp)
        resampled, latent_grad, media_grad, up_g, down_t, *parts = outs
        return (
            resampled.reshape(lead + (lat, half)),
            latent_grad.reshape(lead + (lat, half)),
            media_grad.reshape(lead + (patches, half)),
            parts[0].T[None],
            parts[1].T[None],
            parts[2].T[None],
            parts[3].T[None],
            up_g[None],
            down_t.T[None],
            *parts[4:],
        )
    came, med_came, parts, down_g, out_g, up_g, norm_part = plain_reduce(
        saved, norm_grads, res, latgrad, dmed, dp
    )
    resampled = jnp.where(section == 0, came, res[..., half:])
    latent_grad = jnp.where(section == 0, latgrad[..., :half], came).astype(F32)
    med_mine = lax.dynamic_index_in_dim(dmed, section, 0, keepdims=False)
    media_grad = med_mine.astype(F32) + med_came.astype(F32)
    return (
        resampled.reshape(lead + (lat, half)),
        latent_grad.reshape(lead + (lat, half)),
        media_grad.reshape(lead + (patches, half)),
        parts[0][None],
        parts[1][None],
        parts[2][None],
        out_g[None],
        up_g[None],
        down_g[None],
        *[norm_part[i][None] for i in range(6)],
    )


def solution(mesh):
    feature = P(None, "dp", None, None, "section")
    weight = P("section", None, None)
    vector = P("section", None)
    in_specs = (feature, feature, P(None, "dp"), feature) + (weight,) * 6 + (vector,) * 6
    out_specs = (feature,) * 3 + (P("section", None, "dp"),) * 6 + (P("section", "dp"),) * 6
    return jax.shard_map(
        local, mesh=mesh, in_specs=in_specs, out_specs=out_specs, check_vma=False
    )
```
